512 devices in a mesh: layer: 8 (over y), row: 8 (over x, core), col: 8 (over z).
Axes of the slice: x: 4, y: 8, z: 8, core: 2. Of those that a mesh axis runs over, the one named last changes fastest.
Arguments:
- density: bfloat16 [8192, 8192], P('row', ('col', 'layer')), may hold values from -0.125 to 0.125
- contributions: bfloat16 [32768, 128, 128], P(('layer', 'row', 'col')), may hold values from -5 to 5
- owners: int32 [32768, 1], P(('layer', 'row', 'col')), may hold values from 0 to 63; in each aligned block of 64 rows (0 to 63, 64 to 127, ...) at most 2 rows name the same one
- slots: int32 [32768], P(('layer', 'row', 'col')), may hold values from 0 to 7
- pattern: int32 [64, 64], replicated, may hold values 0 or 1
Outputs:
- product: bfloat16 [8192, 8192], P(('row', 'layer'), 'col')
The draws below stay inside these ranges and needn't reach their ends.
Inputs may be any that keep to these rules, and one draw needn't show every extreme that they name: `owners`: within the rows of one device no owner is named by more than 2 rows; some owner is named by exactly 2.
All inputs are finite; a program needn't handle non-finite values.
Results may differ from the reference program's by a relative error of at most 0.017.
Values may be sent and summed in bfloat16 or wider, within the bound.
No kernel may reach another device: no remote copies, remote signals or barrier semaphores. Data moves between devices by JAX's collectives and lax.ppermute only.
A program may use at most 64 MiB of HBM per device.

```python
import math
import jax
import jax.numpy as jnp
import numpy as np
from jax import lax

TILE = 128
STRIP = 128
NNZ = 16
TR = 8
NC = 64
NT = 64
NW = 8192
KW = 128
SLOTS = 8
CAP = 2
CONTRIB = 32768
N_LAYER = 8
N_ROW = 8
N_COL = 8


def set_ends(values, key, low, largest):
    shape = values.shape
    place = [jax.random.randint(jax.random.fold_in(key, axis), (), 0, shape[axis]) for axis in range(len(shape))]
    values = values.at[tuple(place)].set(low)
    longest = shape.index(max(shape))
    place[longest] = (place[longest] + 1) % shape[longest]
    return values.at[tuple(place)].set(largest)


def block_scale(rng, dims, split, low, largest):
    def one(axis_at, blocks):
        heights = jax.random.uniform(jax.random.fold_in(jax.random.fold_in(rng, 6), axis_at), (blocks,), jnp.float32, low / len(split), largest / len(split))
        return jnp.repeat(jnp.exp(heights), dims[axis_at] // blocks).reshape((-1,) + (1,) * (len(dims) - axis_at - 1))

    level = one(*split[0])
    for cut in split[1:]:
        level = level * one(*cut)
    return level


def shared_out(stream_key, own, number, rows, amount, top, limit, slope):
    order = jax.random.permutation(stream_key, amount)
    crowded, ordinary = load_shares(amount, rows * top, limit, slope, True), load_shares(amount, rows * top, limit, slope, False)
    places = jnp.arange(amount)

    def named(lengths, turn):
        used = int((lengths > 0).sum())
        fixed = max(1, used // 4)
        passed = fixed + (places - fixed + turn * (used - fixed)) % max(1, amount - fixed)
        return jnp.zeros((amount,), jnp.int32).at[order[jnp.where(places < fixed, places, passed)]].set(jnp.asarray(lengths, jnp.int32))

    lengths = jnp.where(number % 4 == 0, named(crowded, number // 4), named(ordinary, number - number // 4 - 1))
    mixed = jax.random.permutation(jax.random.fold_in(own, 3), amount)
    source_of, receiver = mixed[0:amount // 2 * 2:2], mixed[1:amount // 2 * 2:2]
    room = jnp.minimum(lengths[source_of] - 1, limit - lengths[receiver]) // 2
    room = jnp.where((source_of == order[0]) | (receiver == order[0]) | (lengths[receiver] == 0), 0, jnp.maximum(room, 0))
    passed = jax.random.randint(jax.random.fold_in(own, 4), (amount // 2,), 0, 1 << 20) % (room + 1)
    lengths = lengths.at[source_of].add(-passed).at[receiver].add(passed)
    items = jnp.searchsorted(jnp.cumsum(lengths), jnp.arange(rows * top), side="right").astype(jnp.int32)
    listing = items.reshape(top, rows).T
    listing = listing[jax.random.permutation(jax.random.fold_in(own, 1), rows)]
    turn = jax.random.randint(jax.random.fold_in(own, 2), (rows, 1), 0, top)
    return jnp.take_along_axis(listing, (jnp.arange(top)[None, :] + turn) % top, axis=1)


def load_shares(amount, total, limit, lean, full):
    portions = [(1 << 20) // math.isqrt(rank ** lean) + 1 for rank in range(1, amount + 1)]
    largest = limit if full else min(limit, max(-(-total // amount), total * portions[0] // sum(portions)))
    least = 1 if total - largest >= amount - 1 else 0
    given, rest = [largest] + [least] * (amount - 1), total - largest - least * (amount - 1)
    while rest > 0:
        candidates = [i for i in range(1, amount) if given[i] < largest] or [i for i in range(1, amount) if given[i] < limit]
        whole, remaining = sum([portions[i] for i in candidates]), rest
        for i in candidates:
            extra = min(limit - given[i], max(1, remaining * portions[i] // whole), rest)
            given[i] = given[i] + extra
            rest = rest - extra
    return np.array(given)


def noise(stream_key, dims, scale, most, cuts=(), kind=jnp.bfloat16):
    array = scale * jax.random.normal(stream_key, dims, jnp.float32)
    if cuts:
        array = array * block_scale(stream_key, dims, cuts, -0.22, 0.18)
    return jnp.clip(array, -most, most).astype(kind)


def setup_inputs(seed: int = 0) -> dict:
    arg_keys = jax.random.split(jax.random.key(seed), 6)
    density = noise(arg_keys[0], (NW, NW), (NNZ * TILE) ** -0.5, 0.125, ((0, 8), (1, 64)))
    contributions = noise(arg_keys[1], (CONTRIB, STRIP, TILE), 0.35, 5.0, ((0, 512),))
    owners_keys = jax.random.split(jax.random.fold_in(arg_keys[2], 1), CONTRIB // NC)
    owners_turns = jax.random.permutation(jax.random.fold_in(arg_keys[2], 3), CONTRIB // NC)
    owners = jax.vmap(lambda own, number: shared_out(jax.random.fold_in(arg_keys[2], 2), own, number, NC, N_ROW * N_COL, 1, CAP, 2))(owners_keys, owners_turns).reshape((CONTRIB, 1))
    slots = set_ends(jax.random.randint(arg_keys[3], (CONTRIB,), 0, SLOTS), jax.random.fold_in(arg_keys[3], 1), 0, SLOTS - 1).astype(jnp.int32)
    pattern = set_ends((jax.random.randint(arg_keys[4], (NT, NT), 0, NT) < NNZ).astype(jnp.int32), jax.random.fold_in(arg_keys[4], 1), 0, 1)
    return dict(density=density, contributions=contributions, owners=owners, slots=slots, pattern=pattern)


def reference(density, contributions, owners, slots, pattern):
    index = jnp.arange(CONTRIB, dtype=jnp.int32)
    device = index // NC
    layer_of = device // (N_ROW * N_COL)
    target = owners[:, 0]
    row_of = target // N_COL
    col_of = target % N_COL
    strip_row = (row_of * N_LAYER + layer_of) * (KW // STRIP) + slots // TR
    tile_col = col_of * TR + slots % TR
    segment = (strip_row * NT + tile_col).astype(jnp.int32)
    flat = contributions.reshape(CONTRIB, STRIP * TILE).astype(jnp.float32)
    summed = jax.ops.segment_sum(flat, segment, num_segments=(NW // STRIP) * NT)
    hamilton = summed.reshape(NW // STRIP, NT, STRIP, TILE).transpose(0, 2, 1, 3).reshape(NW, NW).astype(jnp.bfloat16)
    keep_tiles = pattern[:, None, :, None]
    sparse = (density.reshape(NT, TILE, NT, TILE) * keep_tiles.astype(jnp.bfloat16)).reshape(NW, NW)
    dens_four = sparse.reshape(NW, N_COL, N_LAYER, KW)
    ham_four = hamilton.reshape(N_ROW, N_LAYER, KW, NW)

    def one_layer(total, layer):
        left = lax.dynamic_index_in_dim(dens_four, layer, 2, keepdims=False).reshape(NW, N_COL * KW)
        right = lax.dynamic_index_in_dim(ham_four, layer, 1, keepdims=False).reshape(N_ROW * KW, NW)
        term = jnp.dot(left, right, preferred_element_type=jnp.float32).astype(jnp.bfloat16)
        term = lax.optimization_barrier(term)
        return total + term.astype(jnp.float32), None

    total, unused = lax.scan(one_layer, jnp.zeros((NW, NW), jnp.float32), jnp.arange(N_LAYER, dtype=jnp.int32))
    kept = total.reshape(NT, TILE, NT, TILE) * keep_tiles.astype(jnp.float32)
    return kept.reshape(NW, NW).astype(jnp.bfloat16)
```

```python
import jax
import jax.numpy as jnp
from jax import lax
from jax.experimental import pallas as pl
from jax.experimental.pallas import tpu as pltpu
from jax.sharding import Mesh, PartitionSpec as P

TILE = 128
SIDE = 8
CAP = 16
BODY = CAP * TILE
META = 16
LAST = TILE - 1
MIB = 1 << 20


def pack_kernel(owners, slots, contributions, out, count, meta, sem, meta_sem):
    for r in range(SIDE):
        count[r] = 0
    row = lax.broadcasted_iota(jnp.int32, (SIDE, TILE), 0)
    lane = lax.broadcasted_iota(jnp.int32, (SIDE, TILE), 1)

    def one(i, places):
        owner = owners[i]
        r = owner // SIDE
        c = owner - r * SIDE
        pos = count[r]
        count[r] = pos + 1
        pltpu.make_async_copy(
            contributions.at[i], out.at[r, pl.ds(pl.multiple_of(pos * TILE, TILE), TILE)], sem
        ).start()
        here = (row == r) & (lane == pos)
        return jnp.where(here, c * SIDE + slots[i], places)

    places = lax.fori_loop(
        0, contributions.shape[0], one, jnp.zeros((SIDE, TILE), jnp.int32), unroll=8
    )
    for r in range(SIDE):
        places = jnp.where((row == r) & (lane == LAST), count[r], places)
    values = places.astype(jnp.float32)
    for r in range(SIDE):
        meta[r] = jnp.broadcast_to(values[r : r + 1], (META, TILE)).astype(jnp.bfloat16)
    tail = pltpu.make_async_copy(meta, out.at[:, pl.ds(BODY, META)], meta_sem)
    tail.start()
    pltpu.make_async_copy(contributions, contributions, sem).wait()
    tail.wait()


def pack(owners, slots, contributions):
    return pl.pallas_call(
        pack_kernel,
        out_shape=jax.ShapeDtypeStruct((SIDE, BODY + META, TILE), jnp.bfloat16),
        in_specs=[
            pl.BlockSpec(memory_space=pltpu.SMEM),
            pl.BlockSpec(memory_space=pltpu.SMEM),
            pl.BlockSpec(memory_space=pl.ANY),
        ],
        out_specs=pl.BlockSpec(memory_space=pl.ANY),
        scratch_shapes=[
            pltpu.SMEM((SIDE,), jnp.int32),
            pltpu.VMEM((SIDE, META, TILE), jnp.bfloat16),
            pltpu.SemaphoreType.DMA,
            pltpu.SemaphoreType.DMA,
        ],
        cost_estimate=pl.CostEstimate(flops=0, bytes_accessed=4 * MIB, transcendentals=0),
        name="pack",
    )(owners, slots, contributions)


def combine_kernel(got, out, data, meta, places, table, total, sems, meta_sem, table_sem):
    head = pltpu.make_async_copy(got.at[:, pl.ds(BODY, META)], meta, meta_sem)
    head.start()
    loads = [
        pltpu.make_async_copy(got.at[r, pl.ds(0, BODY)], data.at[r], sems.at[r])
        for r in range(SIDE)
    ]
    for load in loads:
        load.start()
    total[...] = jnp.zeros_like(total)
    head.wait()
    for r in range(SIDE):
        places[r : r + 1] = meta[r].astype(jnp.float32)[:1].astype(jnp.int32)
    listing = pltpu.make_async_copy(places, table, table_sem)
    listing.start()
    listing.wait()
    for r in range(SIDE):
        loads[r].wait()

        def one(pos, carry, r=r):
            place = table[r, pos]
            rows = pl.ds(pl.multiple_of(pos * TILE, TILE), TILE)
            total[place] += data[r, rows].astype(jnp.float32)
            return carry

        lax.fori_loop(0, table[r, LAST], one, 0)

    def write(c, carry):
        for s in range(SIDE):
            out[c, :, s * TILE : (s + 1) * TILE] = total[c * SIDE + s].astype(jnp.bfloat16)
        return carry

    lax.fori_loop(0, SIDE, write, 0)


def combine(got):
    return pl.pallas_call(
        combine_kernel,
        out_shape=jax.ShapeDtypeStruct((SIDE, TILE, SIDE * TILE), jnp.bfloat16),
        in_specs=[pl.BlockSpec(memory_space=pl.ANY)],
        out_specs=pl.BlockSpec(memory_space=pltpu.VMEM),
        scratch_shapes=[
            pltpu.VMEM((SIDE, BODY, TILE), jnp.bfloat16),
            pltpu.VMEM((SIDE, META, TILE), jnp.bfloat16),
            pltpu.VMEM((SIDE, TILE), jnp.int32),
            pltpu.SMEM((SIDE, TILE), jnp.int32),
            pltpu.VMEM((SIDE * SIDE, TILE, TILE), jnp.float32),
            pltpu.SemaphoreType.DMA((SIDE,)),
            pltpu.SemaphoreType.DMA,
            pltpu.SemaphoreType.DMA,
        ],
        compiler_params=pltpu.CompilerParams(vmem_limit_bytes=24 * MIB),
        cost_estimate=pl.CostEstimate(
            flops=4 * MIB, bytes_accessed=6 * MIB, transcendentals=0
        ),
        name="combine",
    )(got)


def product_kernel(at, near, far, own, other, out, ham):
    half = near.shape[1]
    core, layer = at[0], at[1]

    @pl.when(pl.program_id(0) == 0)
    def _():
        for l in range(2):
            base = jnp.where(layer == l, 0, half)
            for j in range(SIDE // 2):
                mine = base + (2 * j + core) * TILE
                theirs = base + (2 * j + 1 - core) * TILE
                ham[pl.ds(pl.multiple_of(mine, TILE), TILE)] = own[l * 4 + j]
                ham[pl.ds(pl.multiple_of(theirs, TILE), TILE)] = other[l * 4 + j]

    total = jnp.dot(near[...], ham[:half], preferred_element_type=jnp.float32)
    total += jnp.dot(far[...], ham[half:], preferred_element_type=jnp.float32)
    out[...] = total.astype(jnp.bfloat16)


def product_of(at, near, far, own, other):
    rows, half = near.shape
    step = 256
    width = own.shape[2]
    return pl.pallas_call(
        product_kernel,
        out_shape=jax.ShapeDtypeStruct((rows, width), jnp.bfloat16),
        grid_spec=pltpu.PrefetchScalarGridSpec(
            num_scalar_prefetch=1,
            grid=(rows // step,),
            in_specs=[
                pl.BlockSpec((step, half), lambda i, at: (i, 0)),
                pl.BlockSpec((step, half), lambda i, at: (i, 0)),
                pl.BlockSpec(own.shape, lambda i, at: (0, 0, 0)),
                pl.BlockSpec(own.shape, lambda i, at: (0, 0, 0)),
            ],
            out_specs=pl.BlockSpec((step, width), lambda i, at: (i, 0)),
            scratch_shapes=[pltpu.VMEM((2 * half, width), jnp.bfloat16)],
        ),
        compiler_params=pltpu.CompilerParams(vmem_limit_bytes=24 * MIB),
        cost_estimate=pl.CostEstimate(
            flops=4 * rows * half * width, bytes_accessed=7 * MIB, transcendentals=0
        ),
        name="product",
    )(at, near, far, own, other)


def body(density, contributions, owners, slots, pattern):
    row_index = lax.axis_index(("rx", "rc"))
    col_index = lax.axis_index("col")
    layer_index = lax.axis_index(("lg", "lq"))
    core = lax.axis_index("rc")
    pair = lax.axis_index("lq")
    rows, inner = density.shape

    density_tiles = lax.dynamic_slice(
        pattern, (row_index * SIDE, col_index * SIDE + layer_index), (SIDE, 1)
    )
    sparse = (
        density.reshape(SIDE, TILE, inner) * density_tiles[:, :, None].astype(jnp.bfloat16)
    ).reshape(rows, inner)
    near = lax.all_gather(sparse, "col", axis=1, tiled=True)

    packed = pack(owners.reshape(-1), slots, contributions)
    got = lax.all_to_all(packed, ("rx", "rc"), split_axis=0, concat_axis=0, tiled=True)
    partial_ham = combine(got).reshape(rows, rows)
    far = lax.ppermute(near, "lq", [(0, 1), (1, 0)])
    ham = lax.psum_scatter(partial_ham, "col", scatter_dimension=0, tiled=True)

    halves = ham.reshape(inner, 2, rows // 2).transpose(1, 0, 2)
    spread = jnp.broadcast_to(halves[:, None], (2, 4, inner, rows // 2)).reshape(
        8, inner, rows // 2
    )
    own = lax.all_to_all(spread, ("lq", "rx"), split_axis=0, concat_axis=0, tiled=True)
    other = lax.ppermute(own, "rc", [(0, 1), (1, 0)])
    at = jnp.stack([core, pair]).astype(jnp.int32)
    term = product_of(at, near, far, own, other)

    terms = lax.all_to_all(
        term.reshape(SIDE, TILE, rows // 2), ("lg", "lq"), split_axis=0, concat_axis=0, tiled=True
    )
    summed = jnp.sum(terms.reshape(4, 2, TILE, rows // 2).astype(jnp.float32), axis=0)
    kept_tiles = lax.dynamic_slice(
        pattern, (row_index * SIDE + layer_index, col_index * SIDE), (1, SIDE)
    )
    mask = jnp.repeat(kept_tiles.reshape(2, 1, SIDE // 2).astype(jnp.float32), TILE, axis=2)
    kept = summed * mask
    return kept.astype(jnp.bfloat16).transpose(1, 0, 2).reshape(inner, rows)


def solution(mesh):
    layers, grid_rows, grid_cols = mesh.devices.shape
    split = Mesh(
        mesh.devices.reshape(layers // 2, 2, grid_rows // 2, 2, grid_cols),
        ("lg", "lq", "rx", "rc", "col"),
    )
    layer, row = ("lg", "lq"), ("rx", "rc")
    return jax.shard_map(
        body,
        mesh=split,
        in_specs=(
            P(row, ("col", *layer)),
            P((*layer, *row, "col"), None, None),
            P((*layer, *row, "col"), None),
            P((*layer, *row, "col")),
            P(),
        ),
        out_specs=P((*row, *layer), "col"),
        check_vma=False,
    )
```

```python
import jax
import jax.numpy as jnp
from jax import lax
from jax.experimental import pallas as pl
from jax.experimental.pallas import tpu as pltpu
from jax.sharding import Mesh, PartitionSpec as P

TILE = 128
SIDE = 8
CAP = 16
BODY = CAP * TILE
META = 16
LAST = TILE - 1
MIB = 1 << 20
VMEM_MIB = 60


def pack_kernel(owners, slots, pattern, contributions, density, out, sparse, count, listed):
    step = pl.program_id(0)
    per = contributions.shape[0]

    @pl.when(step == 0)
    def _():
        for r in range(SIDE):
            count[r] = 0
        listed[...] = jnp.zeros_like(listed)

    row = lax.broadcasted_iota(jnp.int32, (SIDE, TILE), 0)
    lane = lax.broadcasted_iota(jnp.int32, (SIDE, TILE), 1)

    def one(i, places):
        index = step * per + i
        owner = owners[index]
        r = owner // SIDE
        c = owner - r * SIDE
        pos = count[r]
        count[r] = pos + 1
        out[r, pl.ds(pl.multiple_of(pos * TILE, TILE), TILE)] = contributions[i]
        here = (row == r) & (lane == pos)
        return jnp.where(here, c * SIDE + slots[index], places)

    listed[...] = lax.fori_loop(0, per, one, listed[...], unroll=True)
    tile_row = lax.axis_index(("rx", "rc")) * SIDE + step
    tile_col = lax.axis_index(("col", "lg", "lq"))
    keep = pattern[tile_row, tile_col].astype(jnp.float32)
    sparse[...] = (density[...].astype(jnp.float32) * keep).astype(jnp.bfloat16)

    @pl.when(step == pl.num_programs(0) - 1)
    def _():
        values = listed[...]
        for r in range(SIDE):
            values = jnp.where((row == r) & (lane == LAST), count[r], values)
        values = values.astype(jnp.float32)
        for r in range(SIDE):
            out[r, BODY:] = jnp.broadcast_to(values[r : r + 1], (META, TILE)).astype(jnp.bfloat16)


def pack(owners, slots, pattern, contributions, density):
    per = contributions.shape[0] // SIDE
    shape = (SIDE, BODY + META, TILE)
    return pl.pallas_call(
        pack_kernel,
        out_shape=(
            jax.ShapeDtypeStruct(shape, jnp.bfloat16),
            jax.ShapeDtypeStruct(density.shape, jnp.bfloat16),
        ),
        grid=(SIDE,),
        in_specs=[
            pl.BlockSpec(memory_space=pltpu.SMEM),
            pl.BlockSpec(memory_space=pltpu.SMEM),
            pl.BlockSpec(memory_space=pltpu.SMEM),
            pl.BlockSpec((per, TILE, TILE), lambda i: (i, 0, 0)),
            pl.BlockSpec((TILE, TILE), lambda i: (i, 0)),
        ],
        out_specs=(
            pl.BlockSpec(shape, lambda i: (0, 0, 0)),
            pl.BlockSpec((TILE, TILE), lambda i: (i, 0)),
        ),
        scratch_shapes=[pltpu.SMEM((SIDE,), jnp.int32), pltpu.VMEM((SIDE, TILE), jnp.int32)],
        compiler_params=pltpu.CompilerParams(vmem_limit_bytes=VMEM_MIB * MIB),
        cost_estimate=pl.CostEstimate(flops=0, bytes_accessed=7 * MIB, transcendentals=0),
        name="pack",
    )(owners, slots, pattern, contributions, density)


def combine_kernel(got, near, out, data, meta, places, table, total, sems, meta_sem, table_sem):
    head = pltpu.make_async_copy(got.at[:, pl.ds(BODY, META)], meta, meta_sem)
    head.start()
    loads = [
        pltpu.make_async_copy(got.at[r, pl.ds(0, BODY)], data.at[r], sems.at[r])
        for r in range(SIDE)
    ]
    for load in loads:
        load.start()
    total[...] = jnp.zeros_like(total)
    head.wait()
    for r in range(SIDE):
        places[r : r + 1] = meta[r].astype(jnp.float32)[:1].astype(jnp.int32)
    listing = pltpu.make_async_copy(places, table, table_sem)
    listing.start()
    listing.wait()
    for r in range(SIDE):
        loads[r].wait()

        def one(pos, carry, r=r):
            place = table[r, pos]
            rows = pl.ds(pl.multiple_of(pos * TILE, TILE), TILE)
            total[place] += data[r, rows].astype(jnp.float32)
            return carry

        lax.fori_loop(0, table[r, LAST], one, 0)

    def write(c, carry):
        for s in range(SIDE):
            columns = slice(s % 4 * TILE, (s % 4 + 1) * TILE)
            out[c, s // 4, :, columns] = total[c * SIDE + s].astype(jnp.bfloat16)
        return carry

    lax.fori_loop(0, SIDE, write, 0)


def combine(got, near):
    return pl.pallas_call(
        combine_kernel,
        out_shape=jax.ShapeDtypeStruct((SIDE, 2, TILE, SIDE * TILE // 2), jnp.bfloat16),
        in_specs=[pl.BlockSpec(memory_space=pl.ANY), pl.BlockSpec(memory_space=pl.ANY)],
        out_specs=pl.BlockSpec(memory_space=pltpu.VMEM),
        scratch_shapes=[
            pltpu.VMEM((SIDE, BODY, TILE), jnp.bfloat16),
            pltpu.VMEM((SIDE, META, TILE), jnp.bfloat16),
            pltpu.VMEM((SIDE, TILE), jnp.int32),
            pltpu.SMEM((SIDE, TILE), jnp.int32),
            pltpu.VMEM((SIDE * SIDE, TILE, TILE), jnp.float32),
            pltpu.SemaphoreType.DMA((SIDE,)),
            pltpu.SemaphoreType.DMA,
            pltpu.SemaphoreType.DMA,
        ],
        compiler_params=pltpu.CompilerParams(vmem_limit_bytes=VMEM_MIB * MIB),
        cost_estimate=pl.CostEstimate(
            flops=4 * MIB, bytes_accessed=6 * MIB, transcendentals=0
        ),
        name="combine",
    )(got, near)


def spread_kernel(ham, far, out):
    for half in range(2):
        rows = ham[half * TILE : (half + 1) * TILE]
        for chip in range(4):
            out[half * 4 + chip] = rows


def spread(ham, far):
    depth, width = ham.shape
    return pl.pallas_call(
        spread_kernel,
        out_shape=jax.ShapeDtypeStruct((SIDE, TILE, width), jnp.bfloat16),
        in_specs=[pl.BlockSpec(memory_space=pltpu.VMEM), pl.BlockSpec(memory_space=pl.ANY)],
        out_specs=pl.BlockSpec(memory_space=pltpu.VMEM),
        compiler_params=pltpu.CompilerParams(vmem_limit_bytes=VMEM_MIB * MIB),
        cost_estimate=pl.CostEstimate(flops=0, bytes_accessed=2 * MIB, transcendentals=0),
        name="spread",
    )(ham, far)


def product_kernel(near, far_top, far_bottom, own, other, out, ham):
    half = near.shape[1]
    core, layer = lax.axis_index("rc"), lax.axis_index("lq")
    step = pl.program_id(0)

    @pl.when(step == 0)
    def _():
        for l in range(2):
            base = jnp.where(layer == l, 0, half)
            for j in range(SIDE // 2):
                mine = base + (2 * j + core) * TILE
                theirs = base + (2 * j + 1 - core) * TILE
                ham[pl.ds(pl.multiple_of(mine, TILE), TILE)] = own[l * 4 + j]
                ham[pl.ds(pl.multiple_of(theirs, TILE), TILE)] = other[l * 4 + j]

    def both(far):
        total = jnp.dot(near[...], ham[:half], preferred_element_type=jnp.float32)
        total += jnp.dot(far[...], ham[half:], preferred_element_type=jnp.float32)
        out[...] = total.astype(jnp.bfloat16)

    @pl.when(step < pl.num_programs(0) // 2)
    def _():
        both(far_top)

    @pl.when(step >= pl.num_programs(0) // 2)
    def _():
        both(far_bottom)


def product_of(near, far_top, far_bottom, own, other):
    rows, half = near.shape
    step = 256
    turn = rows // step // 2
    width = own.shape[2]
    return pl.pallas_call(
        product_kernel,
        out_shape=jax.ShapeDtypeStruct((rows, width), jnp.bfloat16),
        grid=(rows // step,),
        in_specs=[
            pl.BlockSpec((step, half), lambda i: (i, 0)),
            pl.BlockSpec((step, half), lambda i: (jnp.minimum(i, turn - 1), 0)),
            pl.BlockSpec((step, half), lambda i: (jnp.maximum(i, turn) - turn, 0)),
            pl.BlockSpec(own.shape, lambda i: (0, 0, 0)),
            pl.BlockSpec(own.shape, lambda i: (0, 0, 0)),
        ],
        out_specs=pl.BlockSpec((step, width), lambda i: (i, 0)),
        scratch_shapes=[pltpu.VMEM((2 * half, width), jnp.bfloat16)],
        compiler_params=pltpu.CompilerParams(vmem_limit_bytes=VMEM_MIB * MIB),
        cost_estimate=pl.CostEstimate(
            flops=4 * rows * half * width, bytes_accessed=7 * MIB, transcendentals=0
        ),
        name="product",
    )(near, far_top, far_bottom, own, other)


def finish_kernel(pattern, terms, out):
    tile_row = lax.axis_index(("rx", "rc", "lg", "lq"))
    tile_col = lax.axis_index("col") * SIDE
    for t in range(SIDE):
        columns = slice(t % 4 * TILE, (t % 4 + 1) * TILE)
        total = jnp.zeros((TILE, TILE), jnp.float32)
        for group in range(4):
            total += terms[group * 2 + t // 4, :, columns].astype(jnp.float32)
        keep = pattern[tile_row, tile_col + t].astype(jnp.float32)
        out[:, t * TILE : (t + 1) * TILE] = (total * keep).astype(jnp.bfloat16)


def finish(pattern, terms):
    return pl.pallas_call(
        finish_kernel,
        out_shape=jax.ShapeDtypeStruct((TILE, SIDE * TILE), jnp.bfloat16),
        in_specs=[
            pl.BlockSpec(memory_space=pltpu.SMEM),
            pl.BlockSpec(memory_space=pltpu.VMEM),
        ],
        out_specs=pl.BlockSpec(memory_space=pltpu.VMEM),
        compiler_params=pltpu.CompilerParams(vmem_limit_bytes=VMEM_MIB * MIB),
        cost_estimate=pl.CostEstimate(flops=MIB, bytes_accessed=2 * MIB, transcendentals=0),
        name="finish",
    )(pattern, terms)


def body(density, contributions, owners, slots, pattern):
    packed, sparse = pack(owners.reshape(-1), slots, pattern, contributions, density)
    near = lax.all_gather(sparse, "col", axis=1, tiled=True)
    got = lax.all_to_all(packed, ("rx", "rc"), split_axis=0, concat_axis=0, tiled=True)
    partial_ham = combine(got, near)
    swap = [(0, 1), (1, 0)]
    rows = near.shape[0]
    far_top = lax.ppermute(near[: rows // 2], "lq", swap)
    far_bottom = lax.ppermute(near[rows // 2 :], "lq", swap)
    depth, width = partial_ham.shape[2:]
    ham = lax.psum_scatter(
        partial_ham.reshape(-1, width), "col", scatter_dimension=0, tiled=True
    )
    own = lax.all_to_all(
        spread(ham, far_top), ("lq", "rx"), split_axis=0, concat_axis=0, tiled=True
    )
    other = lax.ppermute(own, "rc", swap)
    term = product_of(near, far_top, far_bottom, own, other)
    terms = lax.all_to_all(
        term.reshape(SIDE, TILE, width), ("lg", "lq"), split_axis=0, concat_axis=0, tiled=True
    )
    return finish(pattern, terms)


def solution(mesh):
    layers, grid_rows, grid_cols = mesh.devices.shape
    split = Mesh(
        mesh.devices.reshape(layers // 2, 2, grid_rows // 2, 2, grid_cols),
        ("lg", "lq", "rx", "rc", "col"),
    )
    layer, row = ("lg", "lq"), ("rx", "rc")
    return jax.shard_map(
        body,
        mesh=split,
        in_specs=(
            P(row, ("col", *layer)),
            P((*layer, *row, "col"), None, None),
            P((*layer, *row, "col"), None),
            P((*layer, *row, "col")),
            P(),
        ),
        out_specs=P((*row, *layer), "col"),
        check_vma=False,
    )
```

```python
import jax
import jax.numpy as jnp
from jax import lax
from jax.experimental import pallas as pl
from jax.experimental.pallas import tpu as pltpu
from jax.sharding import Mesh, PartitionSpec as P

TILE = 128
SIDE = 8
CAP = 16
BODY = CAP * TILE
META = 16
LAST = TILE - 1
MIB = 1 << 20
VMEM_MIB = 60
SMALL_MIB = 20


def pack_kernel(
    owners, slots, pattern, contributions, density, out, masked, data, meta, count, sems, sem, meta_sem
):
    per = contributions.shape[0] // SIDE
    loads = [
        pltpu.make_async_copy(
            contributions.at[pl.ds(k * per, per)], data.at[pl.ds(k * per, per)], sems.at[k]
        )
        for k in range(SIDE)
    ]
    for load in loads:
        load.start()
    tile_row = lax.axis_index(("rx", "rc")) * SIDE
    tile_col = lax.axis_index(("ch", "cl", "lg", "lq"))
    for t in range(SIDE):
        rows = slice(t * TILE, (t + 1) * TILE)
        keep = pattern[tile_row + t, tile_col].astype(jnp.float32)
        masked[rows] = (density[rows].astype(jnp.float32) * keep).astype(jnp.bfloat16)
        count[t] = 0
    row = lax.broadcasted_iota(jnp.int32, (SIDE, TILE), 0)
    lane = lax.broadcasted_iota(jnp.int32, (SIDE, TILE), 1)
    places = jnp.zeros((SIDE, TILE), jnp.int32)
    for k in range(SIDE):
        loads[k].wait()

        def one(i, places, k=k):
            index = k * per + i
            owner = owners[index]
            r = owner // SIDE
            c = owner - r * SIDE
            pos = count[r]
            count[r] = pos + 1
            pltpu.make_async_copy(
                data.at[index], out.at[r, pl.ds(pl.multiple_of(pos * TILE, TILE), TILE)], sem
            ).start()
            here = (row == r) & (lane == pos)
            return jnp.where(here, c * SIDE + slots[index], places)

        places = lax.fori_loop(0, per, one, places, unroll=True)
    for r in range(SIDE):
        places = jnp.where((row == r) & (lane == LAST), count[r], places)
    values = places.astype(jnp.float32)
    for r in range(SIDE):
        meta[r] = jnp.broadcast_to(values[r : r + 1], (META, TILE)).astype(jnp.bfloat16)
    tail = pltpu.make_async_copy(meta, out.at[:, pl.ds(BODY, META)], meta_sem)
    tail.start()
    tail.wait()
    pltpu.make_async_copy(data, data, sem).wait()


def pack(owners, slots, pattern, contributions, density):
    return pl.pallas_call(
        pack_kernel,
        out_shape=(
            jax.ShapeDtypeStruct((SIDE, BODY + META, TILE), jnp.bfloat16),
            jax.ShapeDtypeStruct(density.shape, jnp.bfloat16),
        ),
        in_specs=[
            pl.BlockSpec(memory_space=pltpu.SMEM),
            pl.BlockSpec(memory_space=pltpu.SMEM),
            pl.BlockSpec(memory_space=pltpu.SMEM),
            pl.BlockSpec(memory_space=pl.ANY),
            pl.BlockSpec(memory_space=pltpu.VMEM),
        ],
        out_specs=(pl.BlockSpec(memory_space=pl.ANY), pl.BlockSpec(memory_space=pltpu.VMEM)),
        scratch_shapes=[
            pltpu.VMEM(contributions.shape, jnp.bfloat16),
            pltpu.VMEM((SIDE, META, TILE), jnp.bfloat16),
            pltpu.SMEM((SIDE,), jnp.int32),
            pltpu.SemaphoreType.DMA((SIDE,)),
            pltpu.SemaphoreType.DMA,
            pltpu.SemaphoreType.DMA,
        ],
        compiler_params=pltpu.CompilerParams(vmem_limit_bytes=VMEM_MIB * MIB),
        cost_estimate=pl.CostEstimate(flops=0, bytes_accessed=7 * MIB, transcendentals=0),
        name="pack",
    )(owners, slots, pattern, contributions, density)


def combine_kernel(got, near, keep, send, data, meta, places, table, total, sems, meta_sem, table_sem):
    head = pltpu.make_async_copy(got.at[:, pl.ds(BODY, META)], meta, meta_sem)
    head.start()
    loads = [
        pltpu.make_async_copy(got.at[r, pl.ds(0, BODY)], data.at[r], sems.at[r])
        for r in range(SIDE)
    ]
    for load in loads:
        load.start()
    total[...] = jnp.zeros_like(total)
    head.wait()
    for r in range(SIDE):
        places[r : r + 1] = meta[r].astype(jnp.float32)[:1].astype(jnp.int32)
    listing = pltpu.make_async_copy(places, table, table_sem)
    listing.start()
    listing.wait()
    for r in range(SIDE):
        loads[r].wait()

        def one(pos, carry, r=r):
            place = table[r, pos]
            rows = pl.ds(pl.multiple_of(pos * TILE, TILE), TILE)
            total[place] += data[r, rows].astype(jnp.float32)
            return carry

        lax.fori_loop(0, table[r, LAST], one, 0)

    parity = lax.axis_index("cl")

    def write(j, carry):
        for s in range(SIDE):
            columns = slice(s % 4 * TILE, (s % 4 + 1) * TILE)
            mine = total[(2 * j + parity) * SIDE + s]
            keep[j, s // 4, :, columns] = mine.astype(jnp.bfloat16)
            theirs = total[(2 * j + 1 - parity) * SIDE + s]
            send[j, s // 4, :, columns] = theirs.astype(jnp.bfloat16)
        return carry

    lax.fori_loop(0, SIDE // 2, write, 0)


def combine(got, near):
    half = jax.ShapeDtypeStruct((SIDE // 2, 2, TILE, SIDE * TILE // 2), jnp.bfloat16)
    return pl.pallas_call(
        combine_kernel,
        out_shape=(half, half),
        in_specs=[pl.BlockSpec(memory_space=pl.ANY), pl.BlockSpec(memory_space=pl.ANY)],
        out_specs=(pl.BlockSpec(memory_space=pltpu.VMEM), pl.BlockSpec(memory_space=pltpu.VMEM)),
        scratch_shapes=[
            pltpu.VMEM((SIDE, BODY, TILE), jnp.bfloat16),
            pltpu.VMEM((SIDE, META, TILE), jnp.bfloat16),
            pltpu.VMEM((SIDE, TILE), jnp.int32),
            pltpu.SMEM((SIDE, TILE), jnp.int32),
            pltpu.VMEM((SIDE * SIDE, TILE, TILE), jnp.float32),
            pltpu.SemaphoreType.DMA((SIDE,)),
            pltpu.SemaphoreType.DMA,
            pltpu.SemaphoreType.DMA,
        ],
        compiler_params=pltpu.CompilerParams(vmem_limit_bytes=VMEM_MIB * MIB),
        cost_estimate=pl.CostEstimate(
            flops=4 * MIB, bytes_accessed=6 * MIB, transcendentals=0
        ),
        name="combine",
    )(got, near)


def spread_kernel(parts, far, out):
    for half in range(2):
        rows = parts[0, half].astype(jnp.float32)
        for part in range(1, parts.shape[0]):
            rows += parts[part, half].astype(jnp.float32)
        rows = rows.astype(jnp.bfloat16)
        for chip in range(4):
            out[half * 4 + chip] = rows


def spread(parts, far):
    depth, width = parts.shape[2:]
    return pl.pallas_call(
        spread_kernel,
        out_shape=jax.ShapeDtypeStruct((SIDE, depth, width), jnp.bfloat16),
        in_specs=[pl.BlockSpec(memory_space=pltpu.VMEM), pl.BlockSpec(memory_space=pl.ANY)],
        out_specs=pl.BlockSpec(memory_space=pltpu.VMEM),
        compiler_params=pltpu.CompilerParams(vmem_limit_bytes=SMALL_MIB * MIB),
        cost_estimate=pl.CostEstimate(flops=MIB, bytes_accessed=2 * MIB, transcendentals=0),
        name="spread",
    )(parts, far)


def product_kernel(near, far, own, other, out, ham):
    half = SIDE * TILE
    core, layer = lax.axis_index("rc"), lax.axis_index("lq")
    column = lax.axis_index(("ch", "cl"))

    @pl.when(pl.program_id(0) == 0)
    def _():
        for l in range(2):
            base = jnp.where(layer == l, 0, half)
            for j in range(SIDE // 2):
                mine = base + (2 * j + core - column + SIDE) % SIDE * TILE
                theirs = base + (2 * j + 1 - core - column + SIDE) % SIDE * TILE
                ham[pl.ds(pl.multiple_of(mine, TILE), TILE)] = own[l * 4 + j]
                ham[pl.ds(pl.multiple_of(theirs, TILE), TILE)] = other[l * 4 + j]

    blocks = [near[c] for c in range(SIDE)] + [far[c] for c in range(SIDE)]
    rows = jnp.concatenate(blocks, axis=1)
    total = jnp.dot(rows, ham[...], preferred_element_type=jnp.float32)
    out[...] = total.astype(jnp.bfloat16)


def product_of(near, far, own, other):
    rows = near.shape[1]
    step = 256
    width = own.shape[2]
    return pl.pallas_call(
        product_kernel,
        out_shape=jax.ShapeDtypeStruct((rows, width), jnp.bfloat16),
        grid=(rows // step,),
        in_specs=[
            pl.BlockSpec((SIDE, step, TILE), lambda i: (0, i, 0)),
            pl.BlockSpec((SIDE, step, TILE), lambda i: (0, i, 0)),
            pl.BlockSpec(own.shape, lambda i: (0, 0, 0)),
            pl.BlockSpec(own.shape, lambda i: (0, 0, 0)),
        ],
        out_specs=pl.BlockSpec((step, width), lambda i: (i, 0)),
        scratch_shapes=[pltpu.VMEM((2 * SIDE * TILE, width), jnp.bfloat16)],
        compiler_params=pltpu.CompilerParams(vmem_limit_bytes=SMALL_MIB * MIB),
        cost_estimate=pl.CostEstimate(
            flops=4 * rows * rows * width, bytes_accessed=7 * MIB, transcendentals=0
        ),
        name="product",
    )(near, far, own, other)


def finish_kernel(pattern, terms, out):
    tile_row = lax.axis_index(("rx", "rc", "lg", "lq"))
    tile_col = lax.axis_index(("ch", "cl")) * SIDE
    for t in range(SIDE):
        columns = slice(t % 4 * TILE, (t % 4 + 1) * TILE)
        total = jnp.zeros((TILE, TILE), jnp.float32)
        for group in range(4):
            total += terms[group * 2 + t // 4, :, columns].astype(jnp.float32)
        keep = pattern[tile_row, tile_col + t].astype(jnp.float32)
        out[:, t * TILE : (t + 1) * TILE] = (total * keep).astype(jnp.bfloat16)


def finish(pattern, terms):
    return pl.pallas_call(
        finish_kernel,
        out_shape=jax.ShapeDtypeStruct((TILE, SIDE * TILE), jnp.bfloat16),
        in_specs=[
            pl.BlockSpec(memory_space=pltpu.SMEM),
            pl.BlockSpec(memory_space=pltpu.VMEM),
        ],
        out_specs=pl.BlockSpec(memory_space=pltpu.VMEM),
        compiler_params=pltpu.CompilerParams(vmem_limit_bytes=SMALL_MIB * MIB),
        cost_estimate=pl.CostEstimate(flops=MIB, bytes_accessed=2 * MIB, transcendentals=0),
        name="finish",
    )(pattern, terms)


def exchange(values, axes):
    return lax.all_to_all(values, axes, split_axis=0, concat_axis=0, tiled=True)


def body(density, contributions, owners, slots, pattern):
    packed, sparse = pack(owners.reshape(-1), slots, pattern, contributions, density)
    got = exchange(packed, ("rx", "rc"))

    def ahead(block, distance):
        return lax.ppermute(
            block, ("ch", "cl"), [(c, (c - distance) % SIDE) for c in range(SIDE)]
        )

    one, last, two, sixth = (ahead(sparse, distance) for distance in (1, -1, 2, -2))
    three, fifth, four = ahead(two, 1), ahead(sixth, -1), ahead(two, 2)
    near = jnp.stack([sparse, one, two, three, four, fifth, sixth, last])
    swap = [(0, 1), (1, 0)]
    far = lax.ppermute(near, "lq", swap)

    keep, send = combine(got, near)
    count = SIDE
    even = [(c, c ^ 1) for c in range(count)]
    odd = [(count + c, count + (c + (1 if c % 2 else -1)) % count) for c in range(count)]
    taken = lax.ppermute(send, ("rc", "ch", "cl"), even + odd)
    parts = exchange(
        (keep.astype(jnp.float32) + taken.astype(jnp.float32)).astype(jnp.bfloat16), "ch"
    )

    own = exchange(spread(parts, far), ("lq", "rx"))
    other = lax.ppermute(own, "rc", swap)
    term = product_of(near, far, own, other)
    terms = exchange(term.reshape(SIDE, TILE, -1), ("lg", "lq"))
    return finish(pattern, terms)


def solution(mesh):
    layers, grid_rows, grid_cols = mesh.devices.shape
    split = Mesh(
        mesh.devices.reshape(layers // 2, 2, grid_rows // 2, 2, grid_cols // 2, 2),
        ("lg", "lq", "rx", "rc", "ch", "cl"),
    )
    layer, row, col = ("lg", "lq"), ("rx", "rc"), ("ch", "cl")
    return jax.shard_map(
        body,
        mesh=split,
        in_specs=(
            P(row, (*col, *layer)),
            P((*layer, *row, *col), None, None),
            P((*layer, *row, *col), None),
            P((*layer, *row, *col)),
            P(),
        ),
        out_specs=P((*row, *layer), col),
        check_vma=False,
    )
```

```python
import jax
import jax.numpy as jnp
from jax import lax
from jax.experimental import pallas as pl
from jax.experimental.pallas import tpu as pltpu
from jax.sharding import Mesh, PartitionSpec as P

TILE = 128
SIDE = 8
CAP = 12
REST = 4
BODY = CAP * TILE
META = 16
LAST = TILE - 1
FLAG = TILE - 2
MIB = 1 << 20
VMEM_MIB = 60
SMALL_MIB = 20


def pack_kernel(
    owners, slots, pattern, contributions, density, out, rest, masked, data, meta, count, sems, sem, meta_sem
):
    per = contributions.shape[0] // SIDE
    loads = [
        pltpu.make_async_copy(
            contributions.at[pl.ds(k * per, per)], data.at[pl.ds(k * per, per)], sems.at[k]
        )
        for k in range(SIDE)
    ]
    for load in loads:
        load.start()
    tile_row = lax.axis_index(("rx", "rc")) * SIDE
    tile_col = lax.axis_index(("ch", "cl", "lg", "lq"))
    for t in range(SIDE):
        rows = slice(t * TILE, (t + 1) * TILE)
        keep = pattern[tile_row + t, tile_col].astype(jnp.float32)
        masked[rows] = (density[rows].astype(jnp.float32) * keep).astype(jnp.bfloat16)
        count[t] = 0
    row = lax.broadcasted_iota(jnp.int32, (SIDE, TILE), 0)
    lane = lax.broadcasted_iota(jnp.int32, (SIDE, TILE), 1)
    places = jnp.zeros((SIDE, TILE), jnp.int32)
    for k in range(SIDE):
        loads[k].wait()

        def one(i, places, k=k):
            index = k * per + i
            owner = owners[index]
            r = owner // SIDE
            c = owner - r * SIDE
            pos = count[r]
            count[r] = pos + 1

            @pl.when(pos < CAP)
            def _():
                at = pl.ds(pl.multiple_of(pos * TILE, TILE), TILE)
                pltpu.make_async_copy(data.at[index], out.at[r, at], sem).start()

            @pl.when(pos >= CAP)
            def _():
                at = pl.ds(pl.multiple_of((pos - CAP) * TILE, TILE), TILE)
                pltpu.make_async_copy(data.at[index], rest.at[r, at], sem).start()

            here = (row == r) & (lane == pos)
            return jnp.where(here, c * SIDE + slots[index], places)

        places = lax.fori_loop(0, per, one, places, unroll=True)
    most = count[0]
    for r in range(1, SIDE):
        most = jnp.maximum(most, count[r])
    places = jnp.where(lane == FLAG, (most > CAP).astype(jnp.int32), places)
    for r in range(SIDE):
        places = jnp.where((row == r) & (lane == LAST), count[r], places)
    values = places.astype(jnp.float32)
    for r in range(SIDE):
        meta[r] = jnp.broadcast_to(values[r : r + 1], (META, TILE)).astype(jnp.bfloat16)
    tail = pltpu.make_async_copy(meta, out.at[:, pl.ds(BODY, META)], meta_sem)
    tail.start()
    tail.wait()
    pltpu.make_async_copy(data, data, sem).wait()


def pack(owners, slots, pattern, contributions, density):
    return pl.pallas_call(
        pack_kernel,
        out_shape=(
            jax.ShapeDtypeStruct((SIDE, BODY + META, TILE), jnp.bfloat16),
            jax.ShapeDtypeStruct((SIDE, REST * TILE, TILE), jnp.bfloat16),
            jax.ShapeDtypeStruct(density.shape, jnp.bfloat16),
        ),
        in_specs=[
            pl.BlockSpec(memory_space=pltpu.SMEM),
            pl.BlockSpec(memory_space=pltpu.SMEM),
            pl.BlockSpec(memory_space=pltpu.SMEM),
            pl.BlockSpec(memory_space=pl.ANY),
            pl.BlockSpec(memory_space=pltpu.VMEM),
        ],
        out_specs=(
            pl.BlockSpec(memory_space=pl.ANY),
            pl.BlockSpec(memory_space=pl.ANY),
            pl.BlockSpec(memory_space=pltpu.VMEM),
        ),
        scratch_shapes=[
            pltpu.VMEM(contributions.shape, jnp.bfloat16),
            pltpu.VMEM((SIDE, META, TILE), jnp.bfloat16),
            pltpu.SMEM((SIDE,), jnp.int32),
            pltpu.SemaphoreType.DMA((SIDE,)),
            pltpu.SemaphoreType.DMA,
            pltpu.SemaphoreType.DMA,
        ],
        compiler_params=pltpu.CompilerParams(vmem_limit_bytes=VMEM_MIB * MIB),
        cost_estimate=pl.CostEstimate(flops=0, bytes_accessed=7 * MIB, transcendentals=0),
        name="pack",
    )(owners, slots, pattern, contributions, density)


def combine_kernel(
    got, more, near, keep, send, data, extra, meta, places, table, total, sems, meta_sem, table_sem, extra_sem
):
    head = pltpu.make_async_copy(got.at[:, pl.ds(BODY, META)], meta, meta_sem)
    head.start()
    loads = [
        pltpu.make_async_copy(got.at[r, pl.ds(0, BODY)], data.at[r], sems.at[r])
        for r in range(SIDE)
    ]
    for load in loads:
        load.start()
    total[...] = jnp.zeros_like(total)
    head.wait()
    for r in range(SIDE):
        places[r : r + 1] = meta[r].astype(jnp.float32)[:1].astype(jnp.int32)
    listing = pltpu.make_async_copy(places, table, table_sem)
    listing.start()
    listing.wait()
    for r in range(SIDE):
        loads[r].wait()

        def one(pos, carry, r=r):
            place = table[r, pos]
            rows = pl.ds(pl.multiple_of(pos * TILE, TILE), TILE)
            total[place] += data[r, rows].astype(jnp.float32)
            return carry

        held = table[r, LAST]
        lax.fori_loop(0, jnp.minimum(held, CAP), one, 0)

        @pl.when(held > CAP)
        def _(r=r, held=held):
            load = pltpu.make_async_copy(more.at[r], extra, extra_sem)
            load.start()
            load.wait()

            def late(pos, carry):
                place = table[r, CAP + pos]
                rows = pl.ds(pl.multiple_of(pos * TILE, TILE), TILE)
                total[place] += extra[rows].astype(jnp.float32)
                return carry

            lax.fori_loop(0, held - CAP, late, 0)


    parity = lax.axis_index("cl")

    def write(j, carry):
        for s in range(SIDE):
            columns = slice(s % 4 * TILE, (s % 4 + 1) * TILE)
            mine = total[(2 * j + parity) * SIDE + s]
            keep[j, s // 4, :, columns] = mine.astype(jnp.bfloat16)
            theirs = total[(2 * j + 1 - parity) * SIDE + s]
            send[j, s // 4, :, columns] = theirs.astype(jnp.bfloat16)
        return carry

    lax.fori_loop(0, SIDE // 2, write, 0)


def combine(got, more, near):
    half = jax.ShapeDtypeStruct((SIDE // 2, 2, TILE, SIDE * TILE // 2), jnp.bfloat16)
    return pl.pallas_call(
        combine_kernel,
        out_shape=(half, half),
        in_specs=[pl.BlockSpec(memory_space=pl.ANY)] * 3,
        out_specs=(pl.BlockSpec(memory_space=pltpu.VMEM), pl.BlockSpec(memory_space=pltpu.VMEM)),
        scratch_shapes=[
            pltpu.VMEM((SIDE, BODY, TILE), jnp.bfloat16),
            pltpu.VMEM((REST * TILE, TILE), jnp.bfloat16),
            pltpu.VMEM((SIDE, META, TILE), jnp.bfloat16),
            pltpu.VMEM((SIDE, TILE), jnp.int32),
            pltpu.SMEM((SIDE, TILE), jnp.int32),
            pltpu.VMEM((SIDE * SIDE, TILE, TILE), jnp.float32),
            pltpu.SemaphoreType.DMA((SIDE,)),
            pltpu.SemaphoreType.DMA,
            pltpu.SemaphoreType.DMA,
            pltpu.SemaphoreType.DMA,
        ],
        compiler_params=pltpu.CompilerParams(vmem_limit_bytes=VMEM_MIB * MIB),
        cost_estimate=pl.CostEstimate(
            flops=4 * MIB, bytes_accessed=6 * MIB, transcendentals=0
        ),
        name="combine",
    )(got, more, near)


def spread_kernel(parts, far, out):
    for half in range(2):
        rows = parts[0, half].astype(jnp.float32)
        for part in range(1, parts.shape[0]):
            rows += parts[part, half].astype(jnp.float32)
        rows = rows.astype(jnp.bfloat16)
        for chip in range(4):
            out[half * 4 + chip] = rows


def spread(parts, far):
    depth, width = parts.shape[2:]
    return pl.pallas_call(
        spread_kernel,
        out_shape=jax.ShapeDtypeStruct((SIDE, depth, width), jnp.bfloat16),
        in_specs=[pl.BlockSpec(memory_space=pltpu.VMEM), pl.BlockSpec(memory_space=pl.ANY)],
        out_specs=pl.BlockSpec(memory_space=pltpu.VMEM),
        compiler_params=pltpu.CompilerParams(vmem_limit_bytes=SMALL_MIB * MIB),
        cost_estimate=pl.CostEstimate(flops=MIB, bytes_accessed=2 * MIB, transcendentals=0),
        name="spread",
    )(parts, far)


def product_kernel(near, far, own, other, out, ham):
    half = SIDE * TILE
    core, layer = lax.axis_index("rc"), lax.axis_index("lq")
    column = lax.axis_index(("ch", "cl"))

    @pl.when(pl.program_id(0) == 0)
    def _():
        for l in range(2):
            base = jnp.where(layer == l, 0, half)
            for j in range(SIDE // 2):
                mine = base + (2 * j + core - column + SIDE) % SIDE * TILE
                theirs = base + (2 * j + 1 - core - column + SIDE) % SIDE * TILE
                ham[pl.ds(pl.multiple_of(mine, TILE), TILE)] = own[l * 4 + j]
                ham[pl.ds(pl.multiple_of(theirs, TILE), TILE)] = other[l * 4 + j]

    blocks = [near[c] for c in range(SIDE)] + [far[c] for c in range(SIDE)]
    rows = jnp.concatenate(blocks, axis=1)
    total = jnp.dot(rows, ham[...], preferred_element_type=jnp.float32)
    out[...] = total.astype(jnp.bfloat16)


def product_of(near, far, own, other):
    rows = near.shape[1]
    step = 256
    width = own.shape[2]
    return pl.pallas_call(
        product_kernel,
        out_shape=jax.ShapeDtypeStruct((rows, width), jnp.bfloat16),
        grid=(rows // step,),
        in_specs=[
            pl.BlockSpec((SIDE, step, TILE), lambda i: (0, i, 0)),
            pl.BlockSpec((SIDE, step, TILE), lambda i: (0, i, 0)),
            pl.BlockSpec(own.shape, lambda i: (0, 0, 0)),
            pl.BlockSpec(own.shape, lambda i: (0, 0, 0)),
        ],
        out_specs=pl.BlockSpec((step, width), lambda i: (i, 0)),
        scratch_shapes=[pltpu.VMEM((2 * SIDE * TILE, width), jnp.bfloat16)],
        compiler_params=pltpu.CompilerParams(vmem_limit_bytes=SMALL_MIB * MIB),
        cost_estimate=pl.CostEstimate(
            flops=4 * rows * rows * width, bytes_accessed=7 * MIB, transcendentals=0
        ),
        name="product",
    )(near, far, own, other)


def finish_kernel(pattern, terms, out):
    tile_row = lax.axis_index(("rx", "rc", "lg", "lq"))
    tile_col = lax.axis_index(("ch", "cl")) * SIDE
    for t in range(SIDE):
        columns = slice(t % 4 * TILE, (t % 4 + 1) * TILE)
        total = jnp.zeros((TILE, TILE), jnp.float32)
        for group in range(4):
            total += terms[group * 2 + t // 4, :, columns].astype(jnp.float32)
        keep = pattern[tile_row, tile_col + t].astype(jnp.float32)
        out[:, t * TILE : (t + 1) * TILE] = (total * keep).astype(jnp.bfloat16)


def finish(pattern, terms):
    return pl.pallas_call(
        finish_kernel,
        out_shape=jax.ShapeDtypeStruct((TILE, SIDE * TILE), jnp.bfloat16),
        in_specs=[
            pl.BlockSpec(memory_space=pltpu.SMEM),
            pl.BlockSpec(memory_space=pltpu.VMEM),
        ],
        out_specs=pl.BlockSpec(memory_space=pltpu.VMEM),
        compiler_params=pltpu.CompilerParams(vmem_limit_bytes=SMALL_MIB * MIB),
        cost_estimate=pl.CostEstimate(flops=MIB, bytes_accessed=2 * MIB, transcendentals=0),
        name="finish",
    )(pattern, terms)


def exchange(values, axes):
    return lax.all_to_all(values, axes, split_axis=0, concat_axis=0, tiled=True)


def body(density, contributions, owners, slots, pattern):
    packed, rest, sparse = pack(owners.reshape(-1), slots, pattern, contributions, density)
    got = exchange(packed, ("rx", "rc"))

    def ahead(block, distance):
        return lax.ppermute(
            block, ("ch", "cl"), [(c, (c - distance) % SIDE) for c in range(SIDE)]
        )

    one, last, two, sixth = (ahead(sparse, distance) for distance in (1, -1, 2, -2))
    three, fifth, four = ahead(two, 1), ahead(sixth, -1), ahead(two, 2)
    near = jnp.stack([sparse, one, two, three, four, fifth, sixth, last])
    swap = [(0, 1), (1, 0)]
    far = lax.ppermute(near, "lq", swap)

    anyone = jnp.max(got[:, BODY, FLAG].astype(jnp.float32)) > 0
    more = lax.cond(anyone, lambda v: exchange(v, ("rx", "rc")), lambda v: v, rest)
    keep, send = combine(got, more, near)
    count = SIDE
    even = [(c, c ^ 1) for c in range(count)]
    odd = [(count + c, count + (c + (1 if c % 2 else -1)) % count) for c in range(count)]
    taken = lax.ppermute(send, ("rc", "ch", "cl"), even + odd)
    parts = exchange(
        (keep.astype(jnp.float32) + taken.astype(jnp.float32)).astype(jnp.bfloat16), "ch"
    )

    own = exchange(spread(parts, far), ("lq", "rx"))
    other = lax.ppermute(own, "rc", swap)
    term = product_of(near, far, own, other)
    terms = exchange(term.reshape(SIDE, TILE, -1), ("lg", "lq"))
    return finish(pattern, terms)


def solution(mesh):
    layers, grid_rows, grid_cols = mesh.devices.shape
    split = Mesh(
        mesh.devices.reshape(layers // 2, 2, grid_rows // 2, 2, grid_cols // 2, 2),
        ("lg", "lq", "rx", "rc", "ch", "cl"),
    )
    layer, row, col = ("lg", "lq"), ("rx", "rc"), ("ch", "cl")
    return jax.shard_map(
        body,
        mesh=split,
        in_specs=(
            P(row, (*col, *layer)),
            P((*layer, *row, *col), None, None),
            P((*layer, *row, *col), None),
            P((*layer, *row, *col)),
            P(),
        ),
        out_specs=P((*row, *layer), col),
        check_vma=False,
    )
```

```python
import functools

import jax
import jax.numpy as jnp
from jax import lax
from jax.experimental import pallas as pl
from jax.experimental.pallas import tpu as pltpu
from jax.sharding import Mesh, PartitionSpec as P

TILE = 128
SIDE = 8
CAP = 12
REST = 4
BODY = CAP * TILE
META = 16
LAST = TILE - 1
FLAG = TILE - 2
MIB = 1 << 20
VMEM_MIB = 60
SMALL_MIB = 20


def pack_kernel(
    owners, slots, pattern, contributions, density, out, rest, masked, data, meta, count, sems, sem, meta_sem
):
    per = contributions.shape[0] // SIDE
    loads = [
        pltpu.make_async_copy(
            contributions.at[pl.ds(k * per, per)], data.at[pl.ds(k * per, per)], sems.at[k]
        )
        for k in range(SIDE)
    ]
    for load in loads:
        load.start()
    tile_row = lax.axis_index(("rx", "rc")) * SIDE
    tile_col = lax.axis_index(("ch", "cl", "lg", "lq"))
    for t in range(SIDE):
        rows = slice(t * TILE, (t + 1) * TILE)
        keep = pattern[tile_row + t, tile_col].astype(jnp.float32)
        masked[rows] = (density[rows].astype(jnp.float32) * keep).astype(jnp.bfloat16)
        count[t] = 0
    row = lax.broadcasted_iota(jnp.int32, (SIDE, TILE), 0)
    lane = lax.broadcasted_iota(jnp.int32, (SIDE, TILE), 1)
    places = jnp.zeros((SIDE, TILE), jnp.int32)
    for k in range(SIDE):
        loads[k].wait()

        def one(i, places, k=k):
            index = k * per + i
            owner = owners[index]
            r = owner // SIDE
            c = owner - r * SIDE
            pos = count[r]
            count[r] = pos + 1

            @pl.when(pos < CAP)
            def _():
                at = pl.ds(pl.multiple_of(pos * TILE, TILE), TILE)
                pltpu.make_async_copy(data.at[index], out.at[r, at], sem).start()

            @pl.when(pos >= CAP)
            def _():
                at = pl.ds(pl.multiple_of((pos - CAP) * TILE, TILE), TILE)
                pltpu.make_async_copy(data.at[index], rest.at[r, at], sem).start()

            here = (row == r) & (lane == pos)
            return jnp.where(here, c * SIDE + slots[index], places)

        places = lax.fori_loop(0, per, one, places, unroll=True)
    most = count[0]
    for r in range(1, SIDE):
        most = jnp.maximum(most, count[r])
    places = jnp.where(lane == FLAG, (most > CAP).astype(jnp.int32), places)
    for r in range(SIDE):
        places = jnp.where((row == r) & (lane == LAST), count[r], places)
    values = places.astype(jnp.float32)
    for r in range(SIDE):
        meta[r] = jnp.broadcast_to(values[r : r + 1], (META, TILE)).astype(jnp.bfloat16)
    tail = pltpu.make_async_copy(meta, out.at[:, pl.ds(BODY, META)], meta_sem)
    tail.start()
    tail.wait()
    pltpu.make_async_copy(data, data, sem).wait()


def pack(owners, slots, pattern, contributions, density):
    return pl.pallas_call(
        pack_kernel,
        out_shape=(
            jax.ShapeDtypeStruct((SIDE, BODY + META, TILE), jnp.bfloat16),
            jax.ShapeDtypeStruct((SIDE, REST * TILE, TILE), jnp.bfloat16),
            jax.ShapeDtypeStruct(density.shape, jnp.bfloat16),
        ),
        in_specs=[
            pl.BlockSpec(memory_space=pltpu.SMEM),
            pl.BlockSpec(memory_space=pltpu.SMEM),
            pl.BlockSpec(memory_space=pltpu.SMEM),
            pl.BlockSpec(memory_space=pl.ANY),
            pl.BlockSpec(memory_space=pltpu.VMEM),
        ],
        out_specs=(
            pl.BlockSpec(memory_space=pl.ANY),
            pl.BlockSpec(memory_space=pl.ANY),
            pl.BlockSpec(memory_space=pltpu.VMEM),
        ),
        scratch_shapes=[
            pltpu.VMEM(contributions.shape, jnp.bfloat16),
            pltpu.VMEM((SIDE, META, TILE), jnp.bfloat16),
            pltpu.SMEM((SIDE,), jnp.int32),
            pltpu.SemaphoreType.DMA((SIDE,)),
            pltpu.SemaphoreType.DMA,
            pltpu.SemaphoreType.DMA,
        ],
        compiler_params=pltpu.CompilerParams(vmem_limit_bytes=VMEM_MIB * MIB),
        cost_estimate=pl.CostEstimate(flops=0, bytes_accessed=7 * MIB, transcendentals=0),
        name="pack",
    )(owners, slots, pattern, contributions, density)


def combine_kernel(
    keeps, got, more, first, out, data, extra, meta, places, table, total, sems, meta_sem, table_sem, extra_sem
):
    head = pltpu.make_async_copy(got.at[:, pl.ds(BODY, META)], meta, meta_sem)
    head.start()
    loads = [
        pltpu.make_async_copy(got.at[r, pl.ds(0, BODY)], data.at[r], sems.at[r])
        for r in range(SIDE)
    ]
    for load in loads:
        load.start()
    total[...] = jnp.zeros_like(total)
    parity = lax.axis_index("cl")
    if not keeps:
        parity = 1 - parity
    head.wait()
    for r in range(SIDE):
        places[r : r + 1] = meta[r].astype(jnp.float32)[:1].astype(jnp.int32)
    listing = pltpu.make_async_copy(places, table, table_sem)
    listing.start()
    listing.wait()

    def put(place, values):
        column = place // SIDE

        @pl.when(column % 2 == parity)
        def _():
            at = column // 2 * SIDE + place % SIDE
            total[at] += values().astype(jnp.float32)

    for r in range(SIDE):
        loads[r].wait()
        held = table[r, LAST]

        def one(pos, carry, r=r):
            rows = pl.ds(pl.multiple_of(pos * TILE, TILE), TILE)
            put(table[r, pos], lambda: data[r, rows])
            return carry

        lax.fori_loop(0, jnp.minimum(held, CAP), one, 0)

        @pl.when(held > CAP)
        def _(r=r, held=held):
            load = pltpu.make_async_copy(more.at[r], extra, extra_sem)
            load.start()
            load.wait()

            def late(pos, carry):
                rows = pl.ds(pl.multiple_of(pos * TILE, TILE), TILE)
                put(table[r, CAP + pos], lambda: extra[rows])
                return carry

            lax.fori_loop(0, held - CAP, late, 0)

    def write(j, carry):
        for s in range(SIDE):
            columns = slice(s % 4 * TILE, (s % 4 + 1) * TILE)
            out[j, s // 4, :, columns] = total[j * SIDE + s].astype(jnp.bfloat16)
        return carry

    lax.fori_loop(0, SIDE // 2, write, 0)


def combine(keeps, got, more, first):
    return pl.pallas_call(
        functools.partial(combine_kernel, keeps),
        out_shape=jax.ShapeDtypeStruct((SIDE // 2, 2, TILE, SIDE * TILE // 2), jnp.bfloat16),
        in_specs=[pl.BlockSpec(memory_space=pl.ANY)] * 3,
        out_specs=pl.BlockSpec(memory_space=pltpu.VMEM),
        scratch_shapes=[
            pltpu.VMEM((SIDE, BODY, TILE), jnp.bfloat16),
            pltpu.VMEM((REST * TILE, TILE), jnp.bfloat16),
            pltpu.VMEM((SIDE, META, TILE), jnp.bfloat16),
            pltpu.VMEM((SIDE, TILE), jnp.int32),
            pltpu.SMEM((SIDE, TILE), jnp.int32),
            pltpu.VMEM((SIDE * SIDE // 2, TILE, TILE), jnp.float32),
            pltpu.SemaphoreType.DMA((SIDE,)),
            pltpu.SemaphoreType.DMA,
            pltpu.SemaphoreType.DMA,
            pltpu.SemaphoreType.DMA,
        ],
        compiler_params=pltpu.CompilerParams(vmem_limit_bytes=SMALL_MIB * MIB),
        cost_estimate=pl.CostEstimate(
            flops=2 * MIB, bytes_accessed=4 * MIB, transcendentals=0
        ),
        name="combine",
    )(got, more, first)


def spread_kernel(parts, far, out):
    for half in range(2):
        rows = parts[0, half].astype(jnp.float32)
        for part in range(1, parts.shape[0]):
            rows += parts[part, half].astype(jnp.float32)
        rows = rows.astype(jnp.bfloat16)
        for chip in range(4):
            out[half * 4 + chip] = rows


def spread(parts, far):
    depth, width = parts.shape[2:]
    return pl.pallas_call(
        spread_kernel,
        out_shape=jax.ShapeDtypeStruct((SIDE, depth, width), jnp.bfloat16),
        in_specs=[pl.BlockSpec(memory_space=pltpu.VMEM), pl.BlockSpec(memory_space=pl.ANY)],
        out_specs=pl.BlockSpec(memory_space=pltpu.VMEM),
        compiler_params=pltpu.CompilerParams(vmem_limit_bytes=SMALL_MIB * MIB),
        cost_estimate=pl.CostEstimate(flops=MIB, bytes_accessed=2 * MIB, transcendentals=0),
        name="spread",
    )(parts, far)


def product_kernel(near, far, own, other, out, ham):
    half = SIDE * TILE
    core, layer = lax.axis_index("rc"), lax.axis_index("lq")
    column = lax.axis_index(("ch", "cl"))

    @pl.when(pl.program_id(0) == 0)
    def _():
        for l in range(2):
            base = jnp.where(layer == l, 0, half)
            for j in range(SIDE // 2):
                mine = base + (2 * j + core - column + SIDE) % SIDE * TILE
                theirs = base + (2 * j + 1 - core - column + SIDE) % SIDE * TILE
                ham[pl.ds(pl.multiple_of(mine, TILE), TILE)] = own[l * 4 + j]
                ham[pl.ds(pl.multiple_of(theirs, TILE), TILE)] = other[l * 4 + j]

    blocks = [near[c] for c in range(SIDE)] + [far[c] for c in range(SIDE)]
    rows = jnp.concatenate(blocks, axis=1)
    total = jnp.dot(rows, ham[...], preferred_element_type=jnp.float32)
    out[...] = total.astype(jnp.bfloat16)


def product_of(near, far, own, other):
    rows = near.shape[1]
    step = 256
    width = own.shape[2]
    return pl.pallas_call(
        product_kernel,
        out_shape=jax.ShapeDtypeStruct((rows, width), jnp.bfloat16),
        grid=(rows // step,),
        in_specs=[
            pl.BlockSpec((SIDE, step, TILE), lambda i: (0, i, 0)),
            pl.BlockSpec((SIDE, step, TILE), lambda i: (0, i, 0)),
            pl.BlockSpec(own.shape, lambda i: (0, 0, 0)),
            pl.BlockSpec(own.shape, lambda i: (0, 0, 0)),
        ],
        out_specs=pl.BlockSpec((step, width), lambda i: (i, 0)),
        scratch_shapes=[pltpu.VMEM((2 * SIDE * TILE, width), jnp.bfloat16)],
        compiler_params=pltpu.CompilerParams(vmem_limit_bytes=SMALL_MIB * MIB),
        cost_estimate=pl.CostEstimate(
            flops=4 * rows * rows * width, bytes_accessed=7 * MIB, transcendentals=0
        ),
        name="product",
    )(near, far, own, other)


def finish_kernel(pattern, terms, out):
    tile_row = lax.axis_index(("rx", "rc", "lg", "lq"))
    tile_col = lax.axis_index(("ch", "cl")) * SIDE
    for t in range(SIDE):
        columns = slice(t % 4 * TILE, (t % 4 + 1) * TILE)
        total = jnp.zeros((TILE, TILE), jnp.float32)
        for group in range(4):
            total += terms[group * 2 + t // 4, :, columns].astype(jnp.float32)
        keep = pattern[tile_row, tile_col + t].astype(jnp.float32)
        out[:, t * TILE : (t + 1) * TILE] = (total * keep).astype(jnp.bfloat16)


def finish(pattern, terms):
    return pl.pallas_call(
        finish_kernel,
        out_shape=jax.ShapeDtypeStruct((TILE, SIDE * TILE), jnp.bfloat16),
        in_specs=[
            pl.BlockSpec(memory_space=pltpu.SMEM),
            pl.BlockSpec(memory_space=pltpu.VMEM),
        ],
        out_specs=pl.BlockSpec(memory_space=pltpu.VMEM),
        compiler_params=pltpu.CompilerParams(vmem_limit_bytes=SMALL_MIB * MIB),
        cost_estimate=pl.CostEstimate(flops=MIB, bytes_accessed=2 * MIB, transcendentals=0),
        name="finish",
    )(pattern, terms)


def exchange(values, axes):
    return lax.all_to_all(values, axes, split_axis=0, concat_axis=0, tiled=True)


def body(density, contributions, owners, slots, pattern):
    packed, rest, sparse = pack(owners.reshape(-1), slots, pattern, contributions, density)
    got = exchange(packed, ("rx", "rc"))

    def ahead(block, distance):
        return lax.ppermute(
            block, ("ch", "cl"), [(c, (c - distance) % SIDE) for c in range(SIDE)]
        )

    one, last, two, sixth = (ahead(sparse, distance) for distance in (1, -1, 2, -2))
    three, fifth, four = ahead(two, 1), ahead(sixth, -1), ahead(two, 2)
    near = jnp.stack([sparse, one, two, three, four, fifth, sixth, last])
    swap = [(0, 1), (1, 0)]
    far = lax.ppermute(near, "lq", swap)

    anyone = jnp.max(got[:, BODY, FLAG].astype(jnp.float32)) > 0
    more = lax.cond(anyone, lambda v: exchange(v, ("rx", "rc")), lambda v: v, rest)
    send = combine(False, got, more, three)
    count = SIDE
    even = [(c, c ^ 1) for c in range(count)]
    odd = [(count + c, count + (c + (1 if c % 2 else -1)) % count) for c in range(count)]
    taken = lax.ppermute(send, ("rc", "ch", "cl"), even + odd)
    keep = combine(True, got, more, near)
    parts = exchange(keep + taken, "ch")

    own = exchange(spread(parts, far), ("lq", "rx"))
    other = lax.ppermute(own, "rc", swap)
    term = product_of(near, far, own, other)
    terms = exchange(term.reshape(SIDE, TILE, -1), ("lg", "lq"))
    return finish(pattern, terms)


def solution(mesh):
    layers, grid_rows, grid_cols = mesh.devices.shape
    split = Mesh(
        mesh.devices.reshape(layers // 2, 2, grid_rows // 2, 2, grid_cols // 2, 2),
        ("lg", "lq", "rx", "rc", "ch", "cl"),
    )
    layer, row, col = ("lg", "lq"), ("rx", "rc"), ("ch", "cl")
    return jax.shard_map(
        body,
        mesh=split,
        in_specs=(
            P(row, (*col, *layer)),
            P((*layer, *row, *col), None, None),
            P((*layer, *row, *col), None),
            P((*layer, *row, *col)),
            P(),
        ),
        out_specs=P((*row, *layer), col),
        check_vma=False,
    )
```

```python
import functools

import jax
import jax.numpy as jnp
from jax import lax
from jax.experimental import pallas as pl
from jax.experimental.pallas import tpu as pltpu
from jax.sharding import Mesh, PartitionSpec as P

TILE = 128
SIDE = 8
CAP = 12
REST = 4
BODY = CAP * TILE
META = 16
LAST = TILE - 1
FLAG = TILE - 2
MIB = 1 << 20
VMEM_MIB = 60
SMALL_MIB = 20


def pack_kernel(
    owners, slots, pattern, contributions, density, out, rest, masked, data, meta, count, sems, sem, meta_sem
):
    per = contributions.shape[0] // SIDE
    loads = [
        pltpu.make_async_copy(
            contributions.at[pl.ds(k * per, per)], data.at[pl.ds(k * per, per)], sems.at[k]
        )
        for k in range(SIDE)
    ]
    for load in loads:
        load.start()
    tile_row = lax.axis_index(("rx", "rc")) * SIDE
    tile_col = lax.axis_index(("ch", "cl", "lg", "lq"))
    for t in range(SIDE):
        rows = slice(t * TILE, (t + 1) * TILE)
        keep = pattern[tile_row + t, tile_col].astype(jnp.float32)
        masked[rows] = (density[rows].astype(jnp.float32) * keep).astype(jnp.bfloat16)
        count[t] = 0
    row = lax.broadcasted_iota(jnp.int32, (SIDE, TILE), 0)
    lane = lax.broadcasted_iota(jnp.int32, (SIDE, TILE), 1)
    places = jnp.zeros((SIDE, TILE), jnp.int32)
    for k in range(SIDE):
        loads[k].wait()

        def one(i, places, k=k):
            index = k * per + i
            owner = owners[index]
            r = owner // SIDE
            c = owner - r * SIDE
            pos = count[r]
            count[r] = pos + 1

            @pl.when(pos < CAP)
            def _():
                at = pl.ds(pl.multiple_of(pos * TILE, TILE), TILE)
                pltpu.make_async_copy(data.at[index], out.at[r, at], sem).start()

            @pl.when(pos >= CAP)
            def _():
                at = pl.ds(pl.multiple_of((pos - CAP) * TILE, TILE), TILE)
                pltpu.make_async_copy(data.at[index], rest.at[r, at], sem).start()

            here = (row == r) & (lane == pos)
            return jnp.where(here, c * SIDE + slots[index], places)

        places = lax.fori_loop(0, per, one, places, unroll=True)
    most = count[0]
    for r in range(1, SIDE):
        most = jnp.maximum(most, count[r])
    places = jnp.where(lane == FLAG, (most > CAP).astype(jnp.int32), places)
    for r in range(SIDE):
        places = jnp.where((row == r) & (lane == LAST), count[r], places)
    values = places.astype(jnp.float32)
    for r in range(SIDE):
        meta[r] = jnp.broadcast_to(values[r : r + 1], (META, TILE)).astype(jnp.bfloat16)
    tail = pltpu.make_async_copy(meta, out.at[:, pl.ds(BODY, META)], meta_sem)
    tail.start()
    tail.wait()
    pltpu.make_async_copy(data, data, sem).wait()


def pack(owners, slots, pattern, contributions, density):
    return pl.pallas_call(
        pack_kernel,
        out_shape=(
            jax.ShapeDtypeStruct((SIDE, BODY + META, TILE), jnp.bfloat16),
            jax.ShapeDtypeStruct((SIDE, REST * TILE, TILE), jnp.bfloat16),
            jax.ShapeDtypeStruct(density.shape, jnp.bfloat16),
        ),
        in_specs=[
            pl.BlockSpec(memory_space=pltpu.SMEM),
            pl.BlockSpec(memory_space=pltpu.SMEM),
            pl.BlockSpec(memory_space=pltpu.SMEM),
            pl.BlockSpec(memory_space=pl.ANY),
            pl.BlockSpec(memory_space=pltpu.VMEM),
        ],
        out_specs=(
            pl.BlockSpec(memory_space=pl.ANY),
            pl.BlockSpec(memory_space=pl.ANY),
            pl.BlockSpec(memory_space=pltpu.VMEM),
        ),
        scratch_shapes=[
            pltpu.VMEM(contributions.shape, jnp.bfloat16),
            pltpu.VMEM((SIDE, META, TILE), jnp.bfloat16),
            pltpu.SMEM((SIDE,), jnp.int32),
            pltpu.SemaphoreType.DMA((SIDE,)),
            pltpu.SemaphoreType.DMA,
            pltpu.SemaphoreType.DMA,
        ],
        compiler_params=pltpu.CompilerParams(vmem_limit_bytes=VMEM_MIB * MIB),
        cost_estimate=pl.CostEstimate(flops=0, bytes_accessed=7 * MIB, transcendentals=0),
        name="pack",
    )(owners, slots, pattern, contributions, density)


def combine_kernel(
    keeps, got, more, first, out, data, extra, meta, places, table, total, sems, meta_sem, table_sem, extra_sem
):
    head = pltpu.make_async_copy(got.at[:, pl.ds(BODY, META)], meta, meta_sem)
    head.start()
    loads = [
        pltpu.make_async_copy(got.at[r, pl.ds(0, BODY)], data.at[r], sems.at[r])
        for r in range(SIDE)
    ]
    for load in loads:
        load.start()
    total[...] = jnp.zeros_like(total)
    parity = lax.axis_index("cl")
    if not keeps:
        parity = 1 - parity
    head.wait()
    for r in range(SIDE):
        places[r : r + 1] = meta[r].astype(jnp.float32)[:1].astype(jnp.int32)
    listing = pltpu.make_async_copy(places, table, table_sem)
    listing.start()
    listing.wait()

    def put(place, values):
        column = place // SIDE

        @pl.when(column % 2 == parity)
        def _():
            at = column // 2 * SIDE + place % SIDE
            total[at] += values().astype(jnp.float32)

    for r in range(SIDE):
        loads[r].wait()
        held = table[r, LAST]

        def one(pos, carry, r=r):
            rows = pl.ds(pl.multiple_of(pos * TILE, TILE), TILE)
            put(table[r, pos], lambda: data[r, rows])
            return carry

        lax.fori_loop(0, jnp.minimum(held, CAP), one, 0)

        @pl.when(held > CAP)
        def _(r=r, held=held):
            load = pltpu.make_async_copy(more.at[r], extra, extra_sem)
            load.start()
            load.wait()

            def late(pos, carry):
                rows = pl.ds(pl.multiple_of(pos * TILE, TILE), TILE)
                put(table[r, CAP + pos], lambda: extra[rows])
                return carry

            lax.fori_loop(0, held - CAP, late, 0)

    def write(j, carry):
        for s in range(SIDE):
            columns = slice(s % 4 * TILE, (s % 4 + 1) * TILE)
            out[j, s // 4, :, columns] = total[j * SIDE + s].astype(jnp.bfloat16)
        return carry

    lax.fori_loop(0, SIDE // 2, write, 0)


def combine(keeps, got, more, first):
    return pl.pallas_call(
        functools.partial(combine_kernel, keeps),
        out_shape=jax.ShapeDtypeStruct((SIDE // 2, 2, TILE, SIDE * TILE // 2), jnp.bfloat16),
        in_specs=[pl.BlockSpec(memory_space=pl.ANY)] * 3,
        out_specs=pl.BlockSpec(memory_space=pltpu.VMEM),
        scratch_shapes=[
            pltpu.VMEM((SIDE, BODY, TILE), jnp.bfloat16),
            pltpu.VMEM((REST * TILE, TILE), jnp.bfloat16),
            pltpu.VMEM((SIDE, META, TILE), jnp.bfloat16),
            pltpu.VMEM((SIDE, TILE), jnp.int32),
            pltpu.SMEM((SIDE, TILE), jnp.int32),
            pltpu.VMEM((SIDE * SIDE // 2, TILE, TILE), jnp.float32),
            pltpu.SemaphoreType.DMA((SIDE,)),
            pltpu.SemaphoreType.DMA,
            pltpu.SemaphoreType.DMA,
            pltpu.SemaphoreType.DMA,
        ],
        compiler_params=pltpu.CompilerParams(vmem_limit_bytes=SMALL_MIB * MIB),
        cost_estimate=pl.CostEstimate(
            flops=2 * MIB, bytes_accessed=4 * MIB, transcendentals=0
        ),
        name="combine",
    )(got, more, first)


def spread_kernel(parts, far, out):
    for half in range(2):
        rows = parts[0, half].astype(jnp.float32)
        for part in range(1, parts.shape[0]):
            rows += parts[part, half].astype(jnp.float32)
        rows = rows.astype(jnp.bfloat16)
        for chip in range(4):
            out[half * 4 + chip] = rows


def spread(parts, far):
    depth, width = parts.shape[2:]
    return pl.pallas_call(
        spread_kernel,
        out_shape=jax.ShapeDtypeStruct((SIDE, depth, width), jnp.bfloat16),
        in_specs=[pl.BlockSpec(memory_space=pltpu.VMEM), pl.BlockSpec(memory_space=pl.ANY)],
        out_specs=pl.BlockSpec(memory_space=pltpu.VMEM),
        compiler_params=pltpu.CompilerParams(vmem_limit_bytes=SMALL_MIB * MIB),
        cost_estimate=pl.CostEstimate(flops=MIB, bytes_accessed=2 * MIB, transcendentals=0),
        name="spread",
    )(parts, far)


def product_kernel(near, near_late, far, far_late, own, other, out, ham):
    half = SIDE * TILE
    core, layer = lax.axis_index("rc"), lax.axis_index("lq")
    column = lax.axis_index(("ch", "cl"))

    def slot(block):
        distance = (block - column + SIDE) % SIDE
        return jnp.where(distance == 7, 3, jnp.where(distance < 3, distance, distance + 1))

    @pl.when(pl.program_id(0) == 0)
    def _():
        for l in range(2):
            base = jnp.where(layer == l, 0, half)
            for j in range(SIDE // 2):
                mine = base + slot(2 * j + core) * TILE
                theirs = base + slot(2 * j + 1 - core) * TILE
                ham[pl.ds(pl.multiple_of(mine, TILE), TILE)] = own[l * 4 + j]
                ham[pl.ds(pl.multiple_of(theirs, TILE), TILE)] = other[l * 4 + j]

    parts = (near, near_late, far, far_late)
    rows = jnp.concatenate([part[c] for part in parts for c in range(SIDE // 2)], axis=1)
    total = jnp.dot(rows, ham[...], preferred_element_type=jnp.float32)
    out[...] = total.astype(jnp.bfloat16)


def product_of(near, near_late, far, far_late, own, other):
    rows = near.shape[1]
    step = 256
    width = own.shape[2]
    block = pl.BlockSpec((SIDE // 2, step, TILE), lambda i: (0, i, 0))
    whole = pl.BlockSpec(own.shape, lambda i: (0, 0, 0))
    return pl.pallas_call(
        product_kernel,
        out_shape=jax.ShapeDtypeStruct((rows, width), jnp.bfloat16),
        grid=(rows // step,),
        in_specs=[block, block, block, block, whole, whole],
        out_specs=pl.BlockSpec((step, width), lambda i: (i, 0)),
        scratch_shapes=[pltpu.VMEM((2 * SIDE * TILE, width), jnp.bfloat16)],
        compiler_params=pltpu.CompilerParams(vmem_limit_bytes=SMALL_MIB * MIB),
        cost_estimate=pl.CostEstimate(
            flops=4 * rows * rows * width, bytes_accessed=7 * MIB, transcendentals=0
        ),
        name="product",
    )(near, near_late, far, far_late, own, other)


def finish_kernel(pattern, terms, out):
    tile_row = lax.axis_index(("rx", "rc", "lg", "lq"))
    tile_col = lax.axis_index(("ch", "cl")) * SIDE
    for t in range(SIDE):
        columns = slice(t % 4 * TILE, (t % 4 + 1) * TILE)
        total = jnp.zeros((TILE, TILE), jnp.float32)
        for group in range(4):
            total += terms[group * 2 + t // 4, :, columns].astype(jnp.float32)
        keep = pattern[tile_row, tile_col + t].astype(jnp.float32)
        out[:, t * TILE : (t + 1) * TILE] = (total * keep).astype(jnp.bfloat16)


def finish(pattern, terms):
    return pl.pallas_call(
        finish_kernel,
        out_shape=jax.ShapeDtypeStruct((TILE, SIDE * TILE), jnp.bfloat16),
        in_specs=[
            pl.BlockSpec(memory_space=pltpu.SMEM),
            pl.BlockSpec(memory_space=pltpu.VMEM),
        ],
        out_specs=pl.BlockSpec(memory_space=pltpu.VMEM),
        compiler_params=pltpu.CompilerParams(vmem_limit_bytes=SMALL_MIB * MIB),
        cost_estimate=pl.CostEstimate(flops=MIB, bytes_accessed=2 * MIB, transcendentals=0),
        name="finish",
    )(pattern, terms)


def exchange(values, axes):
    return lax.all_to_all(values, axes, split_axis=0, concat_axis=0, tiled=True)


def body(density, contributions, owners, slots, pattern):
    packed, rest, sparse = pack(owners.reshape(-1), slots, pattern, contributions, density)
    got = exchange(packed, ("rx", "rc"))

    def ahead(block, distance):
        return lax.ppermute(
            block, ("ch", "cl"), [(c, (c - distance) % SIDE) for c in range(SIDE)]
        )

    one, last, two, sixth = (ahead(sparse, distance) for distance in (1, -1, 2, -2))
    three, fifth, four = ahead(two, 1), ahead(sixth, -1), ahead(two, 2)
    swap = [(0, 1), (1, 0)]
    near = jnp.stack([sparse, one, two, last])
    far = lax.ppermute(near, "lq", swap)
    near_late = jnp.stack([three, four, fifth, sixth])
    far_late = lax.ppermute(near_late, "lq", swap)

    anyone = jnp.max(got[:, BODY, FLAG].astype(jnp.float32)) > 0
    more = lax.cond(anyone, lambda v: exchange(v, ("rx", "rc")), lambda v: v, rest)
    send = combine(False, got, more, near_late)
    count = SIDE
    even = [(c, c ^ 1) for c in range(count)]
    odd = [(count + c, count + (c + (1 if c % 2 else -1)) % count) for c in range(count)]
    taken = lax.ppermute(send, ("rc", "ch", "cl"), even + odd)
    keep = combine(True, got, more, far)
    parts = exchange(keep + taken, "ch")

    own = exchange(spread(parts, far_late), ("lq", "rx"))
    other = lax.ppermute(own, "rc", swap)
    term = product_of(near, near_late, far, far_late, own, other)
    terms = exchange(term.reshape(SIDE, TILE, -1), ("lg", "lq"))
    return finish(pattern, terms)


def solution(mesh):
    layers, grid_rows, grid_cols = mesh.devices.shape
    split = Mesh(
        mesh.devices.reshape(layers // 2, 2, grid_rows // 2, 2, grid_cols // 2, 2),
        ("lg", "lq", "rx", "rc", "ch", "cl"),
    )
    layer, row, col = ("lg", "lq"), ("rx", "rc"), ("ch", "cl")
    return jax.shard_map(
        body,
        mesh=split,
        in_specs=(
            P(row, (*col, *layer)),
            P((*layer, *row, *col), None, None),
            P((*layer, *row, *col), None),
            P((*layer, *row, *col)),
            P(),
        ),
        out_specs=P((*row, *layer), col),
        check_vma=False,
    )
```

```python
import functools

import jax
import jax.numpy as jnp
from jax import lax
from jax.experimental import pallas as pl
from jax.experimental.pallas import tpu as pltpu
from jax.sharding import Mesh, PartitionSpec as P

TILE = 128
SIDE = 8
CAP = 12
REST = 4
BODY = CAP * TILE
META = 16
LAST = TILE - 1
FLAG = TILE - 2
MIB = 1 << 20
VMEM_MIB = 60
SMALL_MIB = 20


def pack_kernel(
    owners, slots, pattern, contributions, density, out, rest, masked, data, meta, count, sems, sem, meta_sem
):
    per = contributions.shape[0] // SIDE
    loads = [
        pltpu.make_async_copy(
            contributions.at[pl.ds(k * per, per)], data.at[pl.ds(k * per, per)], sems.at[k]
        )
        for k in range(SIDE)
    ]
    for load in loads:
        load.start()
    tile_row = lax.axis_index(("rx", "rc")) * SIDE
    tile_col = lax.axis_index(("ch", "cl", "lg", "lq"))
    for t in range(SIDE):
        rows = slice(t * TILE, (t + 1) * TILE)
        keep = pattern[tile_row + t, tile_col].astype(jnp.float32)
        masked[rows] = (density[rows].astype(jnp.float32) * keep).astype(jnp.bfloat16)
        count[t] = 0
    row = lax.broadcasted_iota(jnp.int32, (SIDE, TILE), 0)
    lane = lax.broadcasted_iota(jnp.int32, (SIDE, TILE), 1)
    places = jnp.zeros((SIDE, TILE), jnp.int32)
    for k in range(SIDE):
        loads[k].wait()

        def one(i, places, k=k):
            index = k * per + i
            owner = owners[index]
            r = owner // SIDE
            c = owner - r * SIDE
            pos = count[r]
            count[r] = pos + 1

            @pl.when(pos < CAP)
            def _():
                at = pl.ds(pl.multiple_of(pos * TILE, TILE), TILE)
                pltpu.make_async_copy(data.at[index], out.at[r, at], sem).start()

            @pl.when(pos >= CAP)
            def _():
                at = pl.ds(pl.multiple_of((pos - CAP) * TILE, TILE), TILE)
                pltpu.make_async_copy(data.at[index], rest.at[r, at], sem).start()

            here = (row == r) & (lane == pos)
            return jnp.where(here, c * SIDE + slots[index], places)

        places = lax.fori_loop(0, per, one, places, unroll=True)
    most = count[0]
    for r in range(1, SIDE):
        most = jnp.maximum(most, count[r])
    places = jnp.where(lane == FLAG, (most > CAP).astype(jnp.int32), places)
    for r in range(SIDE):
        places = jnp.where((row == r) & (lane == LAST), count[r], places)
    values = places.astype(jnp.float32)
    for r in range(SIDE):
        meta[r] = jnp.broadcast_to(values[r : r + 1], (META, TILE)).astype(jnp.bfloat16)
    tail = pltpu.make_async_copy(meta, out.at[:, pl.ds(BODY, META)], meta_sem)
    tail.start()
    tail.wait()
    pltpu.make_async_copy(data, data, sem).wait()


def pack(owners, slots, pattern, contributions, density):
    return pl.pallas_call(
        pack_kernel,
        out_shape=(
            jax.ShapeDtypeStruct((SIDE, BODY + META, TILE), jnp.bfloat16),
            jax.ShapeDtypeStruct((SIDE, REST * TILE, TILE), jnp.bfloat16),
            jax.ShapeDtypeStruct(density.shape, jnp.bfloat16),
        ),
        in_specs=[
            pl.BlockSpec(memory_space=pltpu.SMEM),
            pl.BlockSpec(memory_space=pltpu.SMEM),
            pl.BlockSpec(memory_space=pltpu.SMEM),
            pl.BlockSpec(memory_space=pl.ANY),
            pl.BlockSpec(memory_space=pltpu.VMEM),
        ],
        out_specs=(
            pl.BlockSpec(memory_space=pl.ANY),
            pl.BlockSpec(memory_space=pl.ANY),
            pl.BlockSpec(memory_space=pltpu.VMEM),
        ),
        scratch_shapes=[
            pltpu.VMEM(contributions.shape, jnp.bfloat16),
            pltpu.VMEM((SIDE, META, TILE), jnp.bfloat16),
            pltpu.SMEM((SIDE,), jnp.int32),
            pltpu.SemaphoreType.DMA((SIDE,)),
            pltpu.SemaphoreType.DMA,
            pltpu.SemaphoreType.DMA,
        ],
        compiler_params=pltpu.CompilerParams(vmem_limit_bytes=VMEM_MIB * MIB),
        cost_estimate=pl.CostEstimate(flops=0, bytes_accessed=7 * MIB, transcendentals=0),
        name="pack",
    )(owners, slots, pattern, contributions, density)


def combine_kernel(
    keeps, got, more, first, second, out, data, extra, meta, places, table, total, sems, meta_sem, table_sem, extra_sem
):
    head = pltpu.make_async_copy(got.at[:, pl.ds(BODY, META)], meta, meta_sem)
    head.start()
    loads = [
        pltpu.make_async_copy(got.at[r, pl.ds(0, BODY)], data.at[r], sems.at[r])
        for r in range(SIDE)
    ]
    for load in loads:
        load.start()
    total[...] = jnp.zeros_like(total)
    parity = lax.axis_index("cl")
    if not keeps:
        parity = 1 - parity
    head.wait()
    for r in range(SIDE):
        places[r : r + 1] = meta[r].astype(jnp.float32)[:1].astype(jnp.int32)
    listing = pltpu.make_async_copy(places, table, table_sem)
    listing.start()
    listing.wait()

    def put(place, values):
        column = place // SIDE

        @pl.when(column % 2 == parity)
        def _():
            at = column // 2 * SIDE + place % SIDE
            total[at] += values().astype(jnp.float32)

    for r in range(SIDE):
        loads[r].wait()
        held = table[r, LAST]

        def one(pos, carry, r=r):
            rows = pl.ds(pl.multiple_of(pos * TILE, TILE), TILE)
            put(table[r, pos], lambda: data[r, rows])
            return carry

        lax.fori_loop(0, jnp.minimum(held, CAP), one, 0)

        @pl.when(held > CAP)
        def _(r=r, held=held):
            load = pltpu.make_async_copy(more.at[r], extra, extra_sem)
            load.start()
            load.wait()

            def late(pos, carry):
                rows = pl.ds(pl.multiple_of(pos * TILE, TILE), TILE)
                put(table[r, CAP + pos], lambda: extra[rows])
                return carry

            lax.fori_loop(0, held - CAP, late, 0)

    def write(j, carry):
        for s in range(SIDE):
            columns = slice(s % 4 * TILE, (s % 4 + 1) * TILE)
            out[j, s // 4, :, columns] = total[j * SIDE + s].astype(jnp.bfloat16)
        return carry

    lax.fori_loop(0, SIDE // 2, write, 0)


def combine(keeps, got, more, first, second):
    return pl.pallas_call(
        functools.partial(combine_kernel, keeps),
        out_shape=jax.ShapeDtypeStruct((SIDE // 2, 2, TILE, SIDE * TILE // 2), jnp.bfloat16),
        in_specs=[pl.BlockSpec(memory_space=pl.ANY)] * 4,
        out_specs=pl.BlockSpec(memory_space=pltpu.VMEM),
        scratch_shapes=[
            pltpu.VMEM((SIDE, BODY, TILE), jnp.bfloat16),
            pltpu.VMEM((REST * TILE, TILE), jnp.bfloat16),
            pltpu.VMEM((SIDE, META, TILE), jnp.bfloat16),
            pltpu.VMEM((SIDE, TILE), jnp.int32),
            pltpu.SMEM((SIDE, TILE), jnp.int32),
            pltpu.VMEM((SIDE * SIDE // 2, TILE, TILE), jnp.float32),
            pltpu.SemaphoreType.DMA((SIDE,)),
            pltpu.SemaphoreType.DMA,
            pltpu.SemaphoreType.DMA,
            pltpu.SemaphoreType.DMA,
        ],
        compiler_params=pltpu.CompilerParams(vmem_limit_bytes=SMALL_MIB * MIB),
        cost_estimate=pl.CostEstimate(
            flops=2 * MIB, bytes_accessed=4 * MIB, transcendentals=0
        ),
        name="combine",
    )(got, more, first, second)


def spread_kernel(parts, far, out):
    for half in range(2):
        rows = parts[0, half].astype(jnp.float32)
        for part in range(1, parts.shape[0]):
            rows += parts[part, half].astype(jnp.float32)
        rows = rows.astype(jnp.bfloat16)
        for chip in range(4):
            out[half * 4 + chip] = rows


def spread(parts, far):
    depth, width = parts.shape[2:]
    return pl.pallas_call(
        spread_kernel,
        out_shape=jax.ShapeDtypeStruct((SIDE, depth, width), jnp.bfloat16),
        in_specs=[pl.BlockSpec(memory_space=pltpu.VMEM), pl.BlockSpec(memory_space=pl.ANY)],
        out_specs=pl.BlockSpec(memory_space=pltpu.VMEM),
        compiler_params=pltpu.CompilerParams(vmem_limit_bytes=SMALL_MIB * MIB),
        cost_estimate=pl.CostEstimate(flops=MIB, bytes_accessed=2 * MIB, transcendentals=0),
        name="spread",
    )(parts, far)


def product_kernel(near, near_late, far, far_late, own, other, out, ham):
    half = SIDE * TILE
    core, layer = lax.axis_index("rc"), lax.axis_index("lq")
    column = lax.axis_index(("ch", "cl"))

    def slot(block):
        distance = (block - column + SIDE) % SIDE
        late = jnp.where(distance < 6, distance + 2, 10 - distance)
        return jnp.where(distance < 3, distance, late)

    @pl.when(pl.program_id(0) == 0)
    def _():
        for l in range(2):
            base = jnp.where(layer == l, 0, half)
            for j in range(SIDE // 2):
                mine = base + slot(2 * j + core) * TILE
                theirs = base + slot(2 * j + 1 - core) * TILE
                ham[pl.ds(pl.multiple_of(mine, TILE), TILE)] = own[l * 4 + j]
                ham[pl.ds(pl.multiple_of(theirs, TILE), TILE)] = other[l * 4 + j]

    parts = (near, near_late, far, far_late)
    rows = jnp.concatenate([part[c] for part in parts for c in range(part.shape[0])], axis=1)
    total = jnp.dot(rows, ham[...], preferred_element_type=jnp.float32)
    out[...] = total.astype(jnp.bfloat16)


def product_of(near, near_late, far, far_late, own, other):
    rows = near.shape[1]
    step = 256
    width = own.shape[2]
    block = pl.BlockSpec((near.shape[0], step, TILE), lambda i: (0, i, 0))
    late = pl.BlockSpec((near_late.shape[0], step, TILE), lambda i: (0, i, 0))
    whole = pl.BlockSpec(own.shape, lambda i: (0, 0, 0))
    return pl.pallas_call(
        product_kernel,
        out_shape=jax.ShapeDtypeStruct((rows, width), jnp.bfloat16),
        grid=(rows // step,),
        in_specs=[block, late, block, late, whole, whole],
        out_specs=pl.BlockSpec((step, width), lambda i: (i, 0)),
        scratch_shapes=[pltpu.VMEM((2 * SIDE * TILE, width), jnp.bfloat16)],
        compiler_params=pltpu.CompilerParams(vmem_limit_bytes=SMALL_MIB * MIB),
        cost_estimate=pl.CostEstimate(
            flops=4 * rows * rows * width, bytes_accessed=7 * MIB, transcendentals=0
        ),
        name="product",
    )(near, near_late, far, far_late, own, other)


def finish_kernel(pattern, terms, out):
    tile_row = lax.axis_index(("rx", "rc", "lg", "lq"))
    tile_col = lax.axis_index(("ch", "cl")) * SIDE
    for t in range(SIDE):
        columns = slice(t % 4 * TILE, (t % 4 + 1) * TILE)
        total = jnp.zeros((TILE, TILE), jnp.float32)
        for group in range(4):
            total += terms[group * 2 + t // 4, :, columns].astype(jnp.float32)
        keep = pattern[tile_row, tile_col + t].astype(jnp.float32)
        out[:, t * TILE : (t + 1) * TILE] = (total * keep).astype(jnp.bfloat16)


def finish(pattern, terms):
    return pl.pallas_call(
        finish_kernel,
        out_shape=jax.ShapeDtypeStruct((TILE, SIDE * TILE), jnp.bfloat16),
        in_specs=[
            pl.BlockSpec(memory_space=pltpu.SMEM),
            pl.BlockSpec(memory_space=pltpu.VMEM),
        ],
        out_specs=pl.BlockSpec(memory_space=pltpu.VMEM),
        compiler_params=pltpu.CompilerParams(vmem_limit_bytes=SMALL_MIB * MIB),
        cost_estimate=pl.CostEstimate(flops=MIB, bytes_accessed=2 * MIB, transcendentals=0),
        name="finish",
    )(pattern, terms)


def exchange(values, axes):
    return lax.all_to_all(values, axes, split_axis=0, concat_axis=0, tiled=True)


def body(density, contributions, owners, slots, pattern):
    packed, rest, sparse = pack(owners.reshape(-1), slots, pattern, contributions, density)
    got = exchange(packed, ("rx", "rc"))

    def ahead(block, distance):
        return lax.ppermute(
            block, ("ch", "cl"), [(c, (c - distance) % SIDE) for c in range(SIDE)]
        )

    one, last, two, sixth = (ahead(sparse, distance) for distance in (1, -1, 2, -2))
    three, fifth, four = ahead(two, 1), ahead(sixth, -1), ahead(two, 2)
    swap = [(0, 1), (1, 0)]
    near = jnp.stack([sparse, one, two, last, sixth])
    far = lax.ppermute(near, "lq", swap)
    near_late = jnp.stack([three, four, fifth])
    far_late = lax.ppermute(near_late, "lq", swap)

    anyone = jnp.max(got[:, BODY, FLAG].astype(jnp.float32)) > 0
    more = lax.cond(anyone, lambda v: exchange(v, ("rx", "rc")), lambda v: v, rest)
    send = combine(False, got, more, three, fifth)
    count = SIDE
    even = [(c, c ^ 1) for c in range(count)]
    odd = [(count + c, count + (c + (1 if c % 2 else -1)) % count) for c in range(count)]
    taken = lax.ppermute(send, ("rc", "ch", "cl"), even + odd)
    keep = combine(True, got, more, far, near_late)
    parts = exchange(keep + taken, "ch")

    own = exchange(spread(parts, far_late), ("lq", "rx"))
    other = lax.ppermute(own, "rc", swap)
    term = product_of(near, near_late, far, far_late, own, other)
    terms = exchange(term.reshape(SIDE, TILE, -1), ("lg", "lq"))
    return finish(pattern, terms)


def solution(mesh):
    layers, grid_rows, grid_cols = mesh.devices.shape
    split = Mesh(
        mesh.devices.reshape(layers // 2, 2, grid_rows // 2, 2, grid_cols // 2, 2),
        ("lg", "lq", "rx", "rc", "ch", "cl"),
    )
    layer, row, col = ("lg", "lq"), ("rx", "rc"), ("ch", "cl")
    return jax.shard_map(
        body,
        mesh=split,
        in_specs=(
            P(row, (*col, *layer)),
            P((*layer, *row, *col), None, None),
            P((*layer, *row, *col), None),
            P((*layer, *row, *col)),
            P(),
        ),
        out_specs=P((*row, *layer), col),
        check_vma=False,
    )
```

```python
import functools

import jax
import jax.numpy as jnp
from jax import lax
from jax.experimental import pallas as pl
from jax.experimental.pallas import tpu as pltpu
from jax.sharding import Mesh, PartitionSpec as P

TILE = 128
SIDE = 8
CAP = 12
REST = 4
BODY = CAP * TILE
META = 16
LAST = TILE - 1
FLAG = TILE - 2
MIB = 1 << 20
VMEM_MIB = 60
SMALL_MIB = 20


def pack_kernel(
    owners, slots, pattern, contributions, density, out, rest, masked, data, meta, count, sems, sem, meta_sem
):
    per = contributions.shape[0] // SIDE
    loads = [
        pltpu.make_async_copy(
            contributions.at[pl.ds(k * per, per)], data.at[pl.ds(k * per, per)], sems.at[k]
        )
        for k in range(SIDE)
    ]
    for load in loads:
        load.start()
    tile_row = lax.axis_index(("rx", "rc")) * SIDE
    tile_col = lax.axis_index(("ch", "cl", "lg", "lq"))
    for t in range(SIDE):
        rows = slice(t * TILE, (t + 1) * TILE)
        keep = pattern[tile_row + t, tile_col].astype(jnp.float32)
        masked[rows] = (density[rows].astype(jnp.float32) * keep).astype(jnp.bfloat16)
        count[t] = 0
    row = lax.broadcasted_iota(jnp.int32, (SIDE, TILE), 0)
    lane = lax.broadcasted_iota(jnp.int32, (SIDE, TILE), 1)
    places = jnp.zeros((SIDE, TILE), jnp.int32)
    for k in range(SIDE):
        loads[k].wait()

        def one(i, places, k=k):
            index = k * per + i
            owner = owners[index]
            r = owner // SIDE
            c = owner - r * SIDE
            pos = count[r]
            count[r] = pos + 1

            @pl.when(pos < CAP)
            def _():
                at = pl.ds(pl.multiple_of(pos * TILE, TILE), TILE)
                pltpu.make_async_copy(data.at[index], out.at[r, at], sem).start()

            @pl.when(pos >= CAP)
            def _():
                at = pl.ds(pl.multiple_of((pos - CAP) * TILE, TILE), TILE)
                pltpu.make_async_copy(data.at[index], rest.at[r, at], sem).start()

            here = (row == r) & (lane == pos)
            return jnp.where(here, c * SIDE + slots[index], places)

        places = lax.fori_loop(0, per, one, places, unroll=True)
    most = count[0]
    for r in range(1, SIDE):
        most = jnp.maximum(most, count[r])
    places = jnp.where(lane == FLAG, (most > CAP).astype(jnp.int32), places)
    for r in range(SIDE):
        places = jnp.where((row == r) & (lane == LAST), count[r], places)
    values = places.astype(jnp.float32)
    for r in range(SIDE):
        meta[r] = jnp.broadcast_to(values[r : r + 1], (META, TILE)).astype(jnp.bfloat16)
    tail = pltpu.make_async_copy(meta, out.at[:, pl.ds(BODY, META)], meta_sem)
    tail.start()
    tail.wait()
    pltpu.make_async_copy(data, data, sem).wait()


def pack(owners, slots, pattern, contributions, density):
    return pl.pallas_call(
        pack_kernel,
        out_shape=(
            jax.ShapeDtypeStruct((SIDE, BODY + META, TILE), jnp.bfloat16),
            jax.ShapeDtypeStruct((SIDE, REST * TILE, TILE), jnp.bfloat16),
            jax.ShapeDtypeStruct(density.shape, jnp.bfloat16),
        ),
        in_specs=[
            pl.BlockSpec(memory_space=pltpu.SMEM),
            pl.BlockSpec(memory_space=pltpu.SMEM),
            pl.BlockSpec(memory_space=pltpu.SMEM),
            pl.BlockSpec(memory_space=pl.ANY),
            pl.BlockSpec(memory_space=pltpu.VMEM),
        ],
        out_specs=(
            pl.BlockSpec(memory_space=pl.ANY),
            pl.BlockSpec(memory_space=pl.ANY),
            pl.BlockSpec(memory_space=pltpu.VMEM),
        ),
        scratch_shapes=[
            pltpu.VMEM(contributions.shape, jnp.bfloat16),
            pltpu.VMEM((SIDE, META, TILE), jnp.bfloat16),
            pltpu.SMEM((SIDE,), jnp.int32),
            pltpu.SemaphoreType.DMA((SIDE,)),
            pltpu.SemaphoreType.DMA,
            pltpu.SemaphoreType.DMA,
        ],
        compiler_params=pltpu.CompilerParams(vmem_limit_bytes=VMEM_MIB * MIB),
        cost_estimate=pl.CostEstimate(flops=0, bytes_accessed=7 * MIB, transcendentals=0),
        name="pack",
    )(owners, slots, pattern, contributions, density)


def combine_kernel(
    keeps, got, more, first, second, third, out, data, extra, meta, places, table, total, sems, meta_sem, table_sem, extra_sem
):
    head = pltpu.make_async_copy(got.at[:, pl.ds(BODY, META)], meta, meta_sem)
    head.start()
    loads = [
        pltpu.make_async_copy(got.at[r, pl.ds(0, BODY)], data.at[r], sems.at[r])
        for r in range(SIDE)
    ]
    for load in loads:
        load.start()
    total[...] = jnp.zeros_like(total)
    parity = lax.axis_index("cl")
    if not keeps:
        parity = 1 - parity
    head.wait()
    for r in range(SIDE):
        places[r : r + 1] = meta[r].astype(jnp.float32)[:1].astype(jnp.int32)
    listing = pltpu.make_async_copy(places, table, table_sem)
    listing.start()
    listing.wait()

    def put(place, values):
        column = place // SIDE

        @pl.when(column % 2 == parity)
        def _():
            at = column // 2 * SIDE + place % SIDE
            total[at] += values().astype(jnp.float32)

    for r in range(SIDE):
        loads[r].wait()
        held = table[r, LAST]

        def one(pos, carry, r=r):
            rows = pl.ds(pl.multiple_of(pos * TILE, TILE), TILE)
            put(table[r, pos], lambda: data[r, rows])
            return carry

        lax.fori_loop(0, jnp.minimum(held, CAP), one, 0)

        @pl.when(held > CAP)
        def _(r=r, held=held):
            load = pltpu.make_async_copy(more.at[r], extra, extra_sem)
            load.start()
            load.wait()

            def late(pos, carry):
                rows = pl.ds(pl.multiple_of(pos * TILE, TILE), TILE)
                put(table[r, CAP + pos], lambda: extra[rows])
                return carry

            lax.fori_loop(0, held - CAP, late, 0)

    def write(j, carry):
        for s in range(SIDE):
            columns = slice(s % 4 * TILE, (s % 4 + 1) * TILE)
            out[j, s // 4, :, columns] = total[j * SIDE + s].astype(jnp.bfloat16)
        return carry

    lax.fori_loop(0, SIDE // 2, write, 0)


def combine(keeps, got, more, *waits):
    return pl.pallas_call(
        functools.partial(combine_kernel, keeps),
        out_shape=jax.ShapeDtypeStruct((SIDE // 2, 2, TILE, SIDE * TILE // 2), jnp.bfloat16),
        in_specs=[pl.BlockSpec(memory_space=pl.ANY)] * 5,
        out_specs=pl.BlockSpec(memory_space=pltpu.VMEM),
        scratch_shapes=[
            pltpu.VMEM((SIDE, BODY, TILE), jnp.bfloat16),
            pltpu.VMEM((REST * TILE, TILE), jnp.bfloat16),
            pltpu.VMEM((SIDE, META, TILE), jnp.bfloat16),
            pltpu.VMEM((SIDE, TILE), jnp.int32),
            pltpu.SMEM((SIDE, TILE), jnp.int32),
            pltpu.VMEM((SIDE * SIDE // 2, TILE, TILE), jnp.float32),
            pltpu.SemaphoreType.DMA((SIDE,)),
            pltpu.SemaphoreType.DMA,
            pltpu.SemaphoreType.DMA,
            pltpu.SemaphoreType.DMA,
        ],
        compiler_params=pltpu.CompilerParams(vmem_limit_bytes=SMALL_MIB * MIB),
        cost_estimate=pl.CostEstimate(
            flops=2 * MIB, bytes_accessed=4 * MIB, transcendentals=0
        ),
        name="combine",
    )(got, more, *waits)


def add_kernel(keep, taken, wait, out):
    out[...] = keep[...] + taken[...]


def add(keep, taken, wait):
    return pl.pallas_call(
        add_kernel,
        out_shape=jax.ShapeDtypeStruct(keep.shape, keep.dtype),
        in_specs=[pl.BlockSpec(memory_space=pltpu.VMEM)] * 2 + [pl.BlockSpec(memory_space=pl.ANY)],
        out_specs=pl.BlockSpec(memory_space=pltpu.VMEM),
        compiler_params=pltpu.CompilerParams(vmem_limit_bytes=SMALL_MIB * MIB),
        cost_estimate=pl.CostEstimate(flops=MIB, bytes_accessed=3 * MIB, transcendentals=0),
        name="add",
    )(keep, taken, wait)


def spread_kernel(parts, far, out):
    for half in range(2):
        rows = parts[0, half].astype(jnp.float32)
        for part in range(1, parts.shape[0]):
            rows += parts[part, half].astype(jnp.float32)
        rows = rows.astype(jnp.bfloat16)
        for chip in range(4):
            out[half * 4 + chip] = rows


def spread(parts, far):
    depth, width = parts.shape[2:]
    return pl.pallas_call(
        spread_kernel,
        out_shape=jax.ShapeDtypeStruct((SIDE, depth, width), jnp.bfloat16),
        in_specs=[pl.BlockSpec(memory_space=pltpu.VMEM), pl.BlockSpec(memory_space=pl.ANY)],
        out_specs=pl.BlockSpec(memory_space=pltpu.VMEM),
        compiler_params=pltpu.CompilerParams(vmem_limit_bytes=SMALL_MIB * MIB),
        cost_estimate=pl.CostEstimate(flops=MIB, bytes_accessed=2 * MIB, transcendentals=0),
        name="spread",
    )(parts, far)


def product_kernel(*refs):
    *parts, own, other, out, ham = refs
    half = SIDE * TILE
    core, layer = lax.axis_index("rc"), lax.axis_index("lq")
    column = lax.axis_index(("ch", "cl"))

    def slot(block):
        distance = (block - column + SIDE) % SIDE
        late = jnp.where(distance < 5, distance + 3, 10 - distance)
        return jnp.where(distance < 3, distance, late)

    @pl.when(pl.program_id(0) == 0)
    def _():
        for l in range(2):
            base = jnp.where(layer == l, 0, half)
            for j in range(SIDE // 2):
                mine = base + slot(2 * j + core) * TILE
                theirs = base + slot(2 * j + 1 - core) * TILE
                ham[pl.ds(pl.multiple_of(mine, TILE), TILE)] = own[l * 4 + j]
                ham[pl.ds(pl.multiple_of(theirs, TILE), TILE)] = other[l * 4 + j]

    rows = jnp.concatenate([part[c] for part in parts for c in range(part.shape[0])], axis=1)
    total = jnp.dot(rows, ham[...], preferred_element_type=jnp.float32)
    out[...] = total.astype(jnp.bfloat16)


def product_of(parts, own, other):
    rows = parts[0].shape[1]
    step = 256
    width = own.shape[2]
    blocks = [pl.BlockSpec((p.shape[0], step, TILE), lambda i: (0, i, 0)) for p in parts]
    whole = pl.BlockSpec(own.shape, lambda i: (0, 0, 0))
    return pl.pallas_call(
        product_kernel,
        out_shape=jax.ShapeDtypeStruct((rows, width), jnp.bfloat16),
        grid=(rows // step,),
        in_specs=[*blocks, whole, whole],
        out_specs=pl.BlockSpec((step, width), lambda i: (i, 0)),
        scratch_shapes=[pltpu.VMEM((2 * SIDE * TILE, width), jnp.bfloat16)],
        compiler_params=pltpu.CompilerParams(vmem_limit_bytes=SMALL_MIB * MIB),
        cost_estimate=pl.CostEstimate(
            flops=4 * rows * rows * width, bytes_accessed=7 * MIB, transcendentals=0
        ),
        name="product",
    )(*parts, own, other)


def finish_kernel(pattern, terms, out):
    tile_row = lax.axis_index(("rx", "rc", "lg", "lq"))
    tile_col = lax.axis_index(("ch", "cl")) * SIDE
    for t in range(SIDE):
        columns = slice(t % 4 * TILE, (t % 4 + 1) * TILE)
        total = jnp.zeros((TILE, TILE), jnp.float32)
        for group in range(4):
            total += terms[group * 2 + t // 4, :, columns].astype(jnp.float32)
        keep = pattern[tile_row, tile_col + t].astype(jnp.float32)
        out[:, t * TILE : (t + 1) * TILE] = (total * keep).astype(jnp.bfloat16)


def finish(pattern, terms):
    return pl.pallas_call(
        finish_kernel,
        out_shape=jax.ShapeDtypeStruct((TILE, SIDE * TILE), jnp.bfloat16),
        in_specs=[
            pl.BlockSpec(memory_space=pltpu.SMEM),
            pl.BlockSpec(memory_space=pltpu.VMEM),
        ],
        out_specs=pl.BlockSpec(memory_space=pltpu.VMEM),
        compiler_params=pltpu.CompilerParams(vmem_limit_bytes=SMALL_MIB * MIB),
        cost_estimate=pl.CostEstimate(flops=MIB, bytes_accessed=2 * MIB, transcendentals=0),
        name="finish",
    )(pattern, terms)


def exchange(values, axes):
    return lax.all_to_all(values, axes, split_axis=0, concat_axis=0, tiled=True)


def body(density, contributions, owners, slots, pattern):
    packed, rest, sparse = pack(owners.reshape(-1), slots, pattern, contributions, density)
    got = exchange(packed, ("rx", "rc"))

    def ahead(block, distance):
        return lax.ppermute(
            block, ("ch", "cl"), [(c, (c - distance) % SIDE) for c in range(SIDE)]
        )

    one, last, two, sixth = (ahead(sparse, distance) for distance in (1, -1, 2, -2))
    three, fifth, four = ahead(two, 1), ahead(sixth, -1), ahead(two, 2)
    swap = [(0, 1), (1, 0)]
    near = jnp.stack([sparse, one, two, last])
    far = lax.ppermute(near, "lq", swap)
    near_mid = jnp.stack([sixth, fifth])
    far_mid = lax.ppermute(near_mid, "lq", swap)
    near_late = jnp.stack([three, four])
    far_late = lax.ppermute(near_late, "lq", swap)

    anyone = jnp.max(got[:, BODY, FLAG].astype(jnp.float32)) > 0
    more = lax.cond(anyone, lambda v: exchange(v, ("rx", "rc")), lambda v: v, rest)
    send = combine(False, got, more, three, four, fifth)
    count = SIDE
    even = [(c, c ^ 1) for c in range(count)]
    odd = [(count + c, count + (c + (1 if c % 2 else -1)) % count) for c in range(count)]
    taken = lax.ppermute(send, ("rc", "ch", "cl"), even + odd)
    keep = combine(True, got, more, far, near_mid, near_late)
    parts = exchange(add(keep, taken, far_mid), "ch")

    own = exchange(spread(parts, far_late), ("lq", "rx"))
    other = lax.ppermute(own, "rc", swap)
    term = product_of((near, near_mid, near_late, far, far_mid, far_late), own, other)
    terms = exchange(term.reshape(SIDE, TILE, -1), ("lg", "lq"))
    return finish(pattern, terms)


def solution(mesh):
    layers, grid_rows, grid_cols = mesh.devices.shape
    split = Mesh(
        mesh.devices.reshape(layers // 2, 2, grid_rows // 2, 2, grid_cols // 2, 2),
        ("lg", "lq", "rx", "rc", "ch", "cl"),
    )
    layer, row, col = ("lg", "lq"), ("rx", "rc"), ("ch", "cl")
    return jax.shard_map(
        body,
        mesh=split,
        in_specs=(
            P(row, (*col, *layer)),
            P((*layer, *row, *col), None, None),
            P((*layer, *row, *col), None),
            P((*layer, *row, *col)),
            P(),
        ),
        out_specs=P((*row, *layer), col),
        check_vma=False,
    )
```

```python
import functools

import jax
import jax.numpy as jnp
from jax import lax
from jax.experimental import pallas as pl
from jax.experimental.pallas import tpu as pltpu
from jax.sharding import Mesh, PartitionSpec as P

TILE = 128
SIDE = 8
CAP = 12
REST = 4
BODY = CAP * TILE
META = 16
LAST = TILE - 1
FLAG = TILE - 2
MIB = 1 << 20
VMEM_MIB = 60
SMALL_MIB = 20


def pack_kernel(
    owners, slots, pattern, contributions, density, out, rest, masked, data, meta, count, sems, sem, meta_sem
):
    per = contributions.shape[0] // SIDE
    loads = [
        pltpu.make_async_copy(
            contributions.at[pl.ds(k * per, per)], data.at[pl.ds(k * per, per)], sems.at[k]
        )
        for k in range(SIDE)
    ]
    for load in loads:
        load.start()
    tile_row = lax.axis_index(("rx", "rc")) * SIDE
    tile_col = lax.axis_index(("ch", "cl", "lg", "lq"))
    for t in range(SIDE):
        rows = slice(t * TILE, (t + 1) * TILE)
        keep = pattern[tile_row + t, tile_col].astype(jnp.float32)
        masked[rows] = (density[rows].astype(jnp.float32) * keep).astype(jnp.bfloat16)
        count[t] = 0
    row = lax.broadcasted_iota(jnp.int32, (SIDE, TILE), 0)
    lane = lax.broadcasted_iota(jnp.int32, (SIDE, TILE), 1)
    places = jnp.zeros((SIDE, TILE), jnp.int32)
    for k in range(SIDE):
        loads[k].wait()

        def one(i, places, k=k):
            index = k * per + i
            owner = owners[index]
            r = owner // SIDE
            c = owner - r * SIDE
            pos = count[r]
            count[r] = pos + 1

            @pl.when(pos < CAP)
            def _():
                at = pl.ds(pl.multiple_of(pos * TILE, TILE), TILE)
                pltpu.make_async_copy(data.at[index], out.at[r, at], sem).start()

            @pl.when(pos >= CAP)
            def _():
                at = pl.ds(pl.multiple_of((pos - CAP) * TILE, TILE), TILE)
                pltpu.make_async_copy(data.at[index], rest.at[r, at], sem).start()

            here = (row == r) & (lane == pos)
            return jnp.where(here, c * SIDE + slots[index], places)

        places = lax.fori_loop(0, per, one, places, unroll=True)
    most = count[0]
    for r in range(1, SIDE):
        most = jnp.maximum(most, count[r])
    places = jnp.where(lane == FLAG, (most > CAP).astype(jnp.int32), places)
    for r in range(SIDE):
        places = jnp.where((row == r) & (lane == LAST), count[r], places)
    values = places.astype(jnp.float32)
    for r in range(SIDE):
        meta[r] = jnp.broadcast_to(values[r : r + 1], (META, TILE)).astype(jnp.bfloat16)
    tail = pltpu.make_async_copy(meta, out.at[:, pl.ds(BODY, META)], meta_sem)
    tail.start()
    tail.wait()
    pltpu.make_async_copy(data, data, sem).wait()


def pack(owners, slots, pattern, contributions, density):
    return pl.pallas_call(
        pack_kernel,
        out_shape=(
            jax.ShapeDtypeStruct((SIDE, BODY + META, TILE), jnp.bfloat16),
            jax.ShapeDtypeStruct((SIDE, REST * TILE, TILE), jnp.bfloat16),
            jax.ShapeDtypeStruct(density.shape, jnp.bfloat16),
        ),
        in_specs=[
            pl.BlockSpec(memory_space=pltpu.SMEM),
            pl.BlockSpec(memory_space=pltpu.SMEM),
            pl.BlockSpec(memory_space=pltpu.SMEM),
            pl.BlockSpec(memory_space=pl.ANY),
            pl.BlockSpec(memory_space=pltpu.VMEM),
        ],
        out_specs=(
            pl.BlockSpec(memory_space=pl.ANY),
            pl.BlockSpec(memory_space=pl.ANY),
            pl.BlockSpec(memory_space=pltpu.VMEM),
        ),
        scratch_shapes=[
            pltpu.VMEM(contributions.shape, jnp.bfloat16),
            pltpu.VMEM((SIDE, META, TILE), jnp.bfloat16),
            pltpu.SMEM((SIDE,), jnp.int32),
            pltpu.SemaphoreType.DMA((SIDE,)),
            pltpu.SemaphoreType.DMA,
            pltpu.SemaphoreType.DMA,
        ],
        compiler_params=pltpu.CompilerParams(vmem_limit_bytes=VMEM_MIB * MIB),
        cost_estimate=pl.CostEstimate(flops=0, bytes_accessed=7 * MIB, transcendentals=0),
        name="pack",
    )(owners, slots, pattern, contributions, density)


def combine_kernel(
    keeps, got, more, first, second, third, out, data, extra, meta, places, table, total, sems, meta_sem, table_sem, extra_sem
):
    head = pltpu.make_async_copy(got.at[:, pl.ds(BODY, META)], meta, meta_sem)
    head.start()
    loads = [
        pltpu.make_async_copy(got.at[r, pl.ds(0, BODY)], data.at[r], sems.at[r])
        for r in range(SIDE)
    ]
    for load in loads:
        load.start()
    total[...] = jnp.zeros_like(total)
    parity = lax.axis_index("cl")
    if not keeps:
        parity = 1 - parity
    head.wait()
    for r in range(SIDE):
        places[r : r + 1] = meta[r].astype(jnp.float32)[:1].astype(jnp.int32)
    listing = pltpu.make_async_copy(places, table, table_sem)
    listing.start()
    listing.wait()

    def put(place, values):
        column = place // SIDE

        @pl.when(column % 2 == parity)
        def _():
            at = column // 2 * SIDE + place % SIDE
            total[at] += values().astype(jnp.float32)

    for r in range(SIDE):
        loads[r].wait()
        held = table[r, LAST]

        def one(pos, carry, r=r):
            rows = pl.ds(pl.multiple_of(pos * TILE, TILE), TILE)
            put(table[r, pos], lambda: data[r, rows])
            return carry

        lax.fori_loop(0, jnp.minimum(held, CAP), one, 0)

        @pl.when(held > CAP)
        def _(r=r, held=held):
            load = pltpu.make_async_copy(more.at[r], extra, extra_sem)
            load.start()
            load.wait()

            def late(pos, carry):
                rows = pl.ds(pl.multiple_of(pos * TILE, TILE), TILE)
                put(table[r, CAP + pos], lambda: extra[rows])
                return carry

            lax.fori_loop(0, held - CAP, late, 0)

    def write(j, carry):
        for s in range(SIDE):
            columns = slice(s % 4 * TILE, (s % 4 + 1) * TILE)
            out[j, s // 4, :, columns] = total[j * SIDE + s].astype(jnp.bfloat16)
        return carry

    lax.fori_loop(0, SIDE // 2, write, 0)


def combine(keeps, got, more, *waits):
    return pl.pallas_call(
        functools.partial(combine_kernel, keeps),
        out_shape=jax.ShapeDtypeStruct((SIDE // 2, 2, TILE, SIDE * TILE // 2), jnp.bfloat16),
        in_specs=[pl.BlockSpec(memory_space=pl.ANY)] * 5,
        out_specs=pl.BlockSpec(memory_space=pltpu.VMEM),
        scratch_shapes=[
            pltpu.VMEM((SIDE, BODY, TILE), jnp.bfloat16),
            pltpu.VMEM((REST * TILE, TILE), jnp.bfloat16),
            pltpu.VMEM((SIDE, META, TILE), jnp.bfloat16),
            pltpu.VMEM((SIDE, TILE), jnp.int32),
            pltpu.SMEM((SIDE, TILE), jnp.int32),
            pltpu.VMEM((SIDE * SIDE // 2, TILE, TILE), jnp.float32),
            pltpu.SemaphoreType.DMA((SIDE,)),
            pltpu.SemaphoreType.DMA,
            pltpu.SemaphoreType.DMA,
            pltpu.SemaphoreType.DMA,
        ],
        compiler_params=pltpu.CompilerParams(vmem_limit_bytes=SMALL_MIB * MIB),
        cost_estimate=pl.CostEstimate(
            flops=2 * MIB, bytes_accessed=4 * MIB, transcendentals=0
        ),
        name="combine",
    )(got, more, *waits)


def add_kernel(keep, taken, wait, out):
    out[...] = keep[...] + taken[...]


def add(keep, taken, wait):
    return pl.pallas_call(
        add_kernel,
        out_shape=jax.ShapeDtypeStruct(keep.shape, keep.dtype),
        in_specs=[pl.BlockSpec(memory_space=pltpu.VMEM)] * 2 + [pl.BlockSpec(memory_space=pl.ANY)],
        out_specs=pl.BlockSpec(memory_space=pltpu.VMEM),
        compiler_params=pltpu.CompilerParams(vmem_limit_bytes=SMALL_MIB * MIB),
        cost_estimate=pl.CostEstimate(flops=MIB, bytes_accessed=3 * MIB, transcendentals=0),
        name="add",
    )(keep, taken, wait)


def spread_kernel(parts, far, out):
    for half in range(2):
        rows = parts[0, half].astype(jnp.float32)
        for part in range(1, parts.shape[0]):
            rows += parts[part, half].astype(jnp.float32)
        rows = rows.astype(jnp.bfloat16)
        for chip in range(4):
            out[half * 4 + chip] = rows


def spread(parts, far):
    depth, width = parts.shape[2:]
    return pl.pallas_call(
        spread_kernel,
        out_shape=jax.ShapeDtypeStruct((SIDE, depth, width), jnp.bfloat16),
        in_specs=[pl.BlockSpec(memory_space=pltpu.VMEM), pl.BlockSpec(memory_space=pl.ANY)],
        out_specs=pl.BlockSpec(memory_space=pltpu.VMEM),
        compiler_params=pltpu.CompilerParams(vmem_limit_bytes=SMALL_MIB * MIB),
        cost_estimate=pl.CostEstimate(flops=MIB, bytes_accessed=2 * MIB, transcendentals=0),
        name="spread",
    )(parts, far)


def product_kernel(*refs):
    *parts, own, other, out, ham = refs
    half = SIDE * TILE
    core, layer = lax.axis_index("rc"), lax.axis_index("lq")
    column = lax.axis_index(("ch", "cl"))

    def slot(block):
        distance = (block - column + SIDE) % SIDE
        late = jnp.where(distance < 5, distance + 3, 10 - distance)
        return jnp.where(distance < 3, distance, late)

    @pl.when(pl.program_id(0) == 0)
    def _():
        for l in range(2):
            base = jnp.where(layer == l, 0, half)
            for j in range(SIDE // 2):
                mine = base + slot(2 * j + core) * TILE
                theirs = base + slot(2 * j + 1 - core) * TILE
                ham[pl.ds(pl.multiple_of(mine, TILE), TILE)] = own[l * 4 + j]
                ham[pl.ds(pl.multiple_of(theirs, TILE), TILE)] = other[l * 4 + j]

    rows = jnp.concatenate([part[c] for part in parts for c in range(part.shape[0])], axis=1)
    total = jnp.dot(rows, ham[...], preferred_element_type=jnp.float32)
    out[...] = total.astype(jnp.bfloat16)


def product_of(parts, own, other):
    rows = parts[0].shape[1]
    step = 256
    width = own.shape[2]
    blocks = [pl.BlockSpec((p.shape[0], step, TILE), lambda i: (0, i, 0)) for p in parts]
    whole = pl.BlockSpec(own.shape, lambda i: (0, 0, 0))
    return pl.pallas_call(
        product_kernel,
        out_shape=jax.ShapeDtypeStruct((rows, width), jnp.bfloat16),
        grid=(rows // step,),
        in_specs=[*blocks, whole, whole],
        out_specs=pl.BlockSpec((step, width), lambda i: (i, 0)),
        scratch_shapes=[pltpu.VMEM((2 * SIDE * TILE, width), jnp.bfloat16)],
        compiler_params=pltpu.CompilerParams(vmem_limit_bytes=SMALL_MIB * MIB),
        cost_estimate=pl.CostEstimate(
            flops=4 * rows * rows * width, bytes_accessed=7 * MIB, transcendentals=0
        ),
        name="product",
    )(*parts, own, other)


def finish_kernel(pattern, terms, out):
    tile_row = lax.axis_index(("rx", "rc", "lg", "lq"))
    tile_col = lax.axis_index(("ch", "cl")) * SIDE
    for t in range(SIDE):
        columns = slice(t % 4 * TILE, (t % 4 + 1) * TILE)
        total = jnp.zeros((TILE, TILE), jnp.float32)
        for group in range(4):
            total += terms[group * 2 + t // 4, :, columns].astype(jnp.float32)
        keep = pattern[tile_row, tile_col + t].astype(jnp.float32)
        out[:, t * TILE : (t + 1) * TILE] = (total * keep).astype(jnp.bfloat16)


def finish(pattern, terms):
    return pl.pallas_call(
        finish_kernel,
        out_shape=jax.ShapeDtypeStruct((TILE, SIDE * TILE), jnp.bfloat16),
        in_specs=[
            pl.BlockSpec(memory_space=pltpu.SMEM),
            pl.BlockSpec(memory_space=pltpu.VMEM),
        ],
        out_specs=pl.BlockSpec(memory_space=pltpu.VMEM),
        compiler_params=pltpu.CompilerParams(vmem_limit_bytes=SMALL_MIB * MIB),
        cost_estimate=pl.CostEstimate(flops=MIB, bytes_accessed=2 * MIB, transcendentals=0),
        name="finish",
    )(pattern, terms)


def exchange(values, axes):
    return lax.all_to_all(values, axes, split_axis=0, concat_axis=0, tiled=True)


def body(density, contributions, owners, slots, pattern):
    packed, rest, sparse = pack(owners.reshape(-1), slots, pattern, contributions, density)
    got = exchange(packed, ("rx", "rc"))

    def ahead(block, distance):
        return lax.ppermute(
            block, ("ch", "cl"), [(c, (c - distance) % SIDE) for c in range(SIDE)]
        )

    one, last, two, sixth = (ahead(sparse, distance) for distance in (1, -1, 2, -2))
    three, fifth = ahead(two, 1), ahead(sixth, -1)
    down = [(c, (c - 2) % SIDE) for c in range(SIDE)]
    up = [(SIDE + c, SIDE + (c + 2) % SIDE) for c in range(SIDE)]
    opposite = jnp.where(lax.axis_index("rc") == 0, two, sixth)
    four = lax.ppermute(opposite, ("rc", "ch", "cl"), down + up)
    swap = [(0, 1), (1, 0)]
    near = jnp.stack([sparse, one, two, last])
    far = lax.ppermute(near, "lq", swap)
    near_mid = jnp.stack([sixth, fifth])
    far_mid = lax.ppermute(near_mid, "lq", swap)
    near_late = jnp.stack([three, four])
    far_late = lax.ppermute(near_late, "lq", swap)

    anyone = jnp.max(got[:, BODY, FLAG].astype(jnp.float32)) > 0
    more = lax.cond(anyone, lambda v: exchange(v, ("rx", "rc")), lambda v: v, rest)
    send = combine(False, got, more, three, four, fifth)
    count = SIDE
    even = [(c, c ^ 1) for c in range(count)]
    odd = [(count + c, count + (c + (1 if c % 2 else -1)) % count) for c in range(count)]
    taken = lax.ppermute(send, ("rc", "ch", "cl"), even + odd)
    keep = combine(True, got, more, far, near_mid, near_late)
    parts = exchange(add(keep, taken, far_mid), "ch")

    own = exchange(spread(parts, far_late), ("lq", "rx"))
    other = lax.ppermute(own, "rc", swap)
    term = product_of((near, near_mid, near_late, far, far_mid, far_late), own, other)
    terms = exchange(term.reshape(SIDE, TILE, -1), ("lg", "lq"))
    return finish(pattern, terms)


def solution(mesh):
    layers, grid_rows, grid_cols = mesh.devices.shape
    split = Mesh(
        mesh.devices.reshape(layers // 2, 2, grid_rows // 2, 2, grid_cols // 2, 2),
        ("lg", "lq", "rx", "rc", "ch", "cl"),
    )
    layer, row, col = ("lg", "lq"), ("rx", "rc"), ("ch", "cl")
    return jax.shard_map(
        body,
        mesh=split,
        in_specs=(
            P(row, (*col, *layer)),
            P((*layer, *row, *col), None, None),
            P((*layer, *row, *col), None),
            P((*layer, *row, *col)),
            P(),
        ),
        out_specs=P((*row, *layer), col),
        check_vma=False,
    )
```

```python
import functools

import jax
import jax.numpy as jnp
from jax import lax
from jax.experimental import pallas as pl
from jax.experimental.pallas import tpu as pltpu
from jax.sharding import Mesh, PartitionSpec as P

TILE = 128
SIDE = 8
CAP = 12
REST = 4
BODY = CAP * TILE
META = 16
LAST = TILE - 1
FLAG = TILE - 2
MIB = 1 << 20
VMEM_MIB = 60
SMALL_MIB = 20


def pack_kernel(
    owners, slots, pattern, contributions, density, out, rest, masked, data, meta, count, sems, sem, meta_sem
):
    per = contributions.shape[0] // SIDE
    loads = [
        pltpu.make_async_copy(
            contributions.at[pl.ds(k * per, per)], data.at[pl.ds(k * per, per)], sems.at[k]
        )
        for k in range(SIDE)
    ]
    for load in loads:
        load.start()
    tile_row = lax.axis_index(("rx", "rc")) * SIDE
    tile_col = lax.axis_index(("ch", "cl", "lg", "lq"))
    for t in range(SIDE):
        rows = slice(t * TILE, (t + 1) * TILE)
        keep = pattern[tile_row + t, tile_col].astype(jnp.float32)
        masked[rows] = (density[rows].astype(jnp.float32) * keep).astype(jnp.bfloat16)
        count[t] = 0
    row = lax.broadcasted_iota(jnp.int32, (SIDE, TILE), 0)
    lane = lax.broadcasted_iota(jnp.int32, (SIDE, TILE), 1)
    places = jnp.zeros((SIDE, TILE), jnp.int32)
    for k in range(SIDE):
        loads[k].wait()

        def one(i, places, k=k):
            index = k * per + i
            owner = owners[index]
            r = owner // SIDE
            c = owner - r * SIDE
            pos = count[r]
            count[r] = pos + 1

            @pl.when(pos < CAP)
            def _():
                at = pl.ds(pl.multiple_of(pos * TILE, TILE), TILE)
                pltpu.make_async_copy(data.at[index], out.at[r, at], sem).start()

            @pl.when(pos >= CAP)
            def _():
                at = pl.ds(pl.multiple_of((pos - CAP) * TILE, TILE), TILE)
                pltpu.make_async_copy(data.at[index], rest.at[r, at], sem).start()

            here = (row == r) & (lane == pos)
            return jnp.where(here, c * SIDE + slots[index], places)

        places = lax.fori_loop(0, per, one, places, unroll=True)
    most = count[0]
    for r in range(1, SIDE):
        most = jnp.maximum(most, count[r])
    places = jnp.where(lane == FLAG, (most > CAP).astype(jnp.int32), places)
    for r in range(SIDE):
        places = jnp.where((row == r) & (lane == LAST), count[r], places)
    values = places.astype(jnp.float32)
    for r in range(SIDE):
        meta[r] = jnp.broadcast_to(values[r : r + 1], (META, TILE)).astype(jnp.bfloat16)
    tail = pltpu.make_async_copy(meta, out.at[:, pl.ds(BODY, META)], meta_sem)
    tail.start()
    tail.wait()
    pltpu.make_async_copy(data, data, sem).wait()


def pack(owners, slots, pattern, contributions, density):
    return pl.pallas_call(
        pack_kernel,
        out_shape=(
            jax.ShapeDtypeStruct((SIDE, BODY + META, TILE), jnp.bfloat16),
            jax.ShapeDtypeStruct((SIDE, REST * TILE, TILE), jnp.bfloat16),
            jax.ShapeDtypeStruct(density.shape, jnp.bfloat16),
        ),
        in_specs=[
            pl.BlockSpec(memory_space=pltpu.SMEM),
            pl.BlockSpec(memory_space=pltpu.SMEM),
            pl.BlockSpec(memory_space=pltpu.SMEM),
            pl.BlockSpec(memory_space=pl.ANY),
            pl.BlockSpec(memory_space=pltpu.VMEM),
        ],
        out_specs=(
            pl.BlockSpec(memory_space=pl.ANY),
            pl.BlockSpec(memory_space=pl.ANY),
            pl.BlockSpec(memory_space=pltpu.VMEM),
        ),
        scratch_shapes=[
            pltpu.VMEM(contributions.shape, jnp.bfloat16),
            pltpu.VMEM((SIDE, META, TILE), jnp.bfloat16),
            pltpu.SMEM((SIDE,), jnp.int32),
            pltpu.SemaphoreType.DMA((SIDE,)),
            pltpu.SemaphoreType.DMA,
            pltpu.SemaphoreType.DMA,
        ],
        compiler_params=pltpu.CompilerParams(vmem_limit_bytes=VMEM_MIB * MIB),
        cost_estimate=pl.CostEstimate(flops=0, bytes_accessed=7 * MIB, transcendentals=0),
        name="pack",
    )(owners, slots, pattern, contributions, density)


def combine_kernel(
    keeps, got, more, first, second, third, out, data, extra, meta, places, table, total, sems, meta_sem, table_sem, extra_sem
):
    head = pltpu.make_async_copy(got.at[:, pl.ds(BODY, META)], meta, meta_sem)
    head.start()
    loads = [
        pltpu.make_async_copy(got.at[r, pl.ds(0, BODY)], data.at[r], sems.at[r])
        for r in range(SIDE)
    ]
    for load in loads:
        load.start()
    total[...] = jnp.zeros_like(total)
    parity = lax.axis_index("cl")
    if not keeps:
        parity = 1 - parity
    head.wait()
    for r in range(SIDE):
        places[r : r + 1] = meta[r].astype(jnp.float32)[:1].astype(jnp.int32)
    listing = pltpu.make_async_copy(places, table, table_sem)
    listing.start()
    listing.wait()

    def put(place, values):
        column = place // SIDE

        @pl.when(column % 2 == parity)
        def _():
            at = column // 2 * SIDE + place % SIDE
            total[at] += values().astype(jnp.float32)

    for r in range(SIDE):
        loads[r].wait()
        held = table[r, LAST]

        def one(pos, carry, r=r):
            rows = pl.ds(pl.multiple_of(pos * TILE, TILE), TILE)
            put(table[r, pos], lambda: data[r, rows])
            return carry

        lax.fori_loop(0, jnp.minimum(held, CAP), one, 0)

        @pl.when(held > CAP)
        def _(r=r, held=held):
            load = pltpu.make_async_copy(more.at[r], extra, extra_sem)
            load.start()
            load.wait()

            def late(pos, carry):
                rows = pl.ds(pl.multiple_of(pos * TILE, TILE), TILE)
                put(table[r, CAP + pos], lambda: extra[rows])
                return carry

            lax.fori_loop(0, held - CAP, late, 0)

    def write(j, carry):
        for s in range(SIDE):
            columns = slice(s % 4 * TILE, (s % 4 + 1) * TILE)
            out[j, s // 4, :, columns] = total[j * SIDE + s].astype(jnp.bfloat16)
        return carry

    lax.fori_loop(0, SIDE // 2, write, 0)


def combine(keeps, got, more, *waits):
    return pl.pallas_call(
        functools.partial(combine_kernel, keeps),
        out_shape=jax.ShapeDtypeStruct((SIDE // 2, 2, TILE, SIDE * TILE // 2), jnp.bfloat16),
        in_specs=[pl.BlockSpec(memory_space=pl.ANY)] * 5,
        out_specs=pl.BlockSpec(memory_space=pltpu.VMEM),
        scratch_shapes=[
            pltpu.VMEM((SIDE, BODY, TILE), jnp.bfloat16),
            pltpu.VMEM((REST * TILE, TILE), jnp.bfloat16),
            pltpu.VMEM((SIDE, META, TILE), jnp.bfloat16),
            pltpu.VMEM((SIDE, TILE), jnp.int32),
            pltpu.SMEM((SIDE, TILE), jnp.int32),
            pltpu.VMEM((SIDE * SIDE // 2, TILE, TILE), jnp.float32),
            pltpu.SemaphoreType.DMA((SIDE,)),
            pltpu.SemaphoreType.DMA,
            pltpu.SemaphoreType.DMA,
            pltpu.SemaphoreType.DMA,
        ],
        compiler_params=pltpu.CompilerParams(vmem_limit_bytes=SMALL_MIB * MIB),
        cost_estimate=pl.CostEstimate(
            flops=2 * MIB, bytes_accessed=4 * MIB, transcendentals=0
        ),
        name="combine",
    )(got, more, *waits)


def add_kernel(keep, taken, wait, out):
    out[...] = keep[...] + taken[...]


def add(keep, taken, wait):
    return pl.pallas_call(
        add_kernel,
        out_shape=jax.ShapeDtypeStruct(keep.shape, keep.dtype),
        in_specs=[pl.BlockSpec(memory_space=pltpu.VMEM)] * 2 + [pl.BlockSpec(memory_space=pl.ANY)],
        out_specs=pl.BlockSpec(memory_space=pltpu.VMEM),
        compiler_params=pltpu.CompilerParams(vmem_limit_bytes=SMALL_MIB * MIB),
        cost_estimate=pl.CostEstimate(flops=MIB, bytes_accessed=3 * MIB, transcendentals=0),
        name="add",
    )(keep, taken, wait)


def spread_kernel(parts, far, out):
    for half in range(2):
        rows = parts[0, half].astype(jnp.float32)
        for part in range(1, parts.shape[0]):
            rows += parts[part, half].astype(jnp.float32)
        rows = rows.astype(jnp.bfloat16)
        for chip in range(4):
            out[half * 4 + chip] = rows


def spread(parts, far):
    depth, width = parts.shape[2:]
    return pl.pallas_call(
        spread_kernel,
        out_shape=jax.ShapeDtypeStruct((SIDE, depth, width), jnp.bfloat16),
        in_specs=[pl.BlockSpec(memory_space=pltpu.VMEM), pl.BlockSpec(memory_space=pl.ANY)],
        out_specs=pl.BlockSpec(memory_space=pltpu.VMEM),
        compiler_params=pltpu.CompilerParams(vmem_limit_bytes=SMALL_MIB * MIB),
        cost_estimate=pl.CostEstimate(flops=MIB, bytes_accessed=2 * MIB, transcendentals=0),
        name="spread",
    )(parts, far)


def product_kernel(*refs):
    *parts, own, other, out, ham = refs
    half = SIDE * TILE
    core, layer = lax.axis_index("rc"), lax.axis_index("lq")
    column = lax.axis_index(("ch", "cl"))

    def slot(block):
        distance = (block - column + SIDE) % SIDE
        late = jnp.where(distance < 5, distance + 3, 10 - distance)
        return jnp.where(distance < 3, distance, late)

    @pl.when(pl.program_id(0) == 0)
    def _():
        for l in range(2):
            base = jnp.where(layer == l, 0, half)
            for j in range(SIDE // 2):
                mine = base + slot(2 * j + core) * TILE
                theirs = base + slot(2 * j + 1 - core) * TILE
                ham[pl.ds(pl.multiple_of(mine, TILE), TILE)] = own[l * 4 + j]
                ham[pl.ds(pl.multiple_of(theirs, TILE), TILE)] = other[l * 4 + j]

    rows = jnp.concatenate([part[c] for part in parts for c in range(part.shape[0])], axis=1)
    total = jnp.dot(rows, ham[...], preferred_element_type=jnp.float32)
    out[...] = total.astype(jnp.bfloat16)


def product_of(parts, own, other):
    rows = parts[0].shape[1]
    step = 256
    width = own.shape[2]
    blocks = [pl.BlockSpec((p.shape[0], step, TILE), lambda i: (0, i, 0)) for p in parts]
    whole = pl.BlockSpec(own.shape, lambda i: (0, 0, 0))
    return pl.pallas_call(
        product_kernel,
        out_shape=jax.ShapeDtypeStruct((rows, width), jnp.bfloat16),
        grid=(rows // step,),
        in_specs=[*blocks, whole, whole],
        out_specs=pl.BlockSpec((step, width), lambda i: (i, 0)),
        scratch_shapes=[pltpu.VMEM((2 * SIDE * TILE, width), jnp.bfloat16)],
        compiler_params=pltpu.CompilerParams(vmem_limit_bytes=SMALL_MIB * MIB),
        cost_estimate=pl.CostEstimate(
            flops=4 * rows * rows * width, bytes_accessed=7 * MIB, transcendentals=0
        ),
        name="product",
    )(*parts, own, other)


def finish_kernel(pattern, terms, out):
    tile_row = lax.axis_index(("rx", "rc", "lg", "lq"))
    tile_col = lax.axis_index(("ch", "cl")) * SIDE
    for t in range(SIDE):
        columns = slice(t % 4 * TILE, (t % 4 + 1) * TILE)
        total = jnp.zeros((TILE, TILE), jnp.float32)
        for group in range(4):
            total += terms[group * 2 + t // 4, :, columns].astype(jnp.float32)
        keep = pattern[tile_row, tile_col + t].astype(jnp.float32)
        out[:, t * TILE : (t + 1) * TILE] = (total * keep).astype(jnp.bfloat16)


def finish(pattern, terms):
    return pl.pallas_call(
        finish_kernel,
        out_shape=jax.ShapeDtypeStruct((TILE, SIDE * TILE), jnp.bfloat16),
        in_specs=[
            pl.BlockSpec(memory_space=pltpu.SMEM),
            pl.BlockSpec(memory_space=pltpu.VMEM),
        ],
        out_specs=pl.BlockSpec(memory_space=pltpu.VMEM),
        compiler_params=pltpu.CompilerParams(vmem_limit_bytes=SMALL_MIB * MIB),
        cost_estimate=pl.CostEstimate(flops=MIB, bytes_accessed=2 * MIB, transcendentals=0),
        name="finish",
    )(pattern, terms)


def exchange(values, axes):
    return lax.all_to_all(values, axes, split_axis=0, concat_axis=0, tiled=True)


def body(density, contributions, owners, slots, pattern):
    packed, rest, sparse = pack(owners.reshape(-1), slots, pattern, contributions, density)
    got = exchange(packed, ("rx", "rc"))

    def ahead(block, distance):
        return lax.ppermute(
            block, ("ch", "cl"), [(c, (c - distance) % SIDE) for c in range(SIDE)]
        )

    one, last, two, sixth = (ahead(sparse, distance) for distance in (1, -1, 2, -2))
    three, fifth = ahead(two, 1), ahead(sixth, -1)
    down = [(c, (c - 2) % SIDE) for c in range(SIDE)]
    up = [(SIDE + c, SIDE + (c + 2) % SIDE) for c in range(SIDE)]
    opposite = jnp.where(lax.axis_index("rc") == 0, two, sixth)
    four = lax.ppermute(opposite, ("rc", "ch", "cl"), down + up)
    swap = [(0, 1), (1, 0)]
    near = jnp.stack([sparse, one, two, last])
    far = lax.ppermute(near, "lq", swap)
    near_late = jnp.stack([sixth, fifth, three, four])
    far_late = lax.ppermute(near_late, "lq", swap)

    anyone = jnp.max(got[:, BODY, FLAG].astype(jnp.float32)) > 0
    more = lax.cond(anyone, lambda v: exchange(v, ("rx", "rc")), lambda v: v, rest)
    send = combine(False, got, more, three, four, fifth)
    count = SIDE
    even = [(c, c ^ 1) for c in range(count)]
    odd = [(count + c, count + (c + (1 if c % 2 else -1)) % count) for c in range(count)]
    taken = lax.ppermute(send, ("rc", "ch", "cl"), even + odd)
    keep = combine(True, got, more, near, near_late, near_late)
    parts = exchange(add(keep, taken, far), "ch")

    own = exchange(spread(parts, far_late), ("lq", "rx"))
    other = lax.ppermute(own, "rc", swap)
    term = product_of((near, near_late, far, far_late), own, other)
    terms = exchange(term.reshape(SIDE, TILE, -1), ("lg", "lq"))
    return finish(pattern, terms)


def solution(mesh):
    layers, grid_rows, grid_cols = mesh.devices.shape
    split = Mesh(
        mesh.devices.reshape(layers // 2, 2, grid_rows // 2, 2, grid_cols // 2, 2),
        ("lg", "lq", "rx", "rc", "ch", "cl"),
    )
    layer, row, col = ("lg", "lq"), ("rx", "rc"), ("ch", "cl")
    return jax.shard_map(
        body,
        mesh=split,
        in_specs=(
            P(row, (*col, *layer)),
            P((*layer, *row, *col), None, None),
            P((*layer, *row, *col), None),
            P((*layer, *row, *col)),
            P(),
        ),
        out_specs=P((*row, *layer), col),
        check_vma=False,
    )
```

```python
import functools

import jax
import jax.numpy as jnp
from jax import lax
from jax.experimental import pallas as pl
from jax.experimental.pallas import tpu as pltpu
from jax.sharding import Mesh, PartitionSpec as P

TILE = 128
SIDE = 8
CAP = 12
REST = 4
BODY = CAP * TILE
META = 16
LAST = TILE - 1
FLAG = TILE - 2
MIB = 1 << 20
VMEM_MIB = 60
SMALL_MIB = 20


def pack_kernel(
    owners, slots, pattern, contributions, density, out, rest, masked, data, meta, count, sems, sem, meta_sem
):
    per = contributions.shape[0] // SIDE
    loads = [
        pltpu.make_async_copy(
            contributions.at[pl.ds(k * per, per)], data.at[pl.ds(k * per, per)], sems.at[k]
        )
        for k in range(SIDE)
    ]
    for load in loads:
        load.start()
    tile_row = lax.axis_index(("rx", "rc")) * SIDE
    tile_col = lax.axis_index(("ch", "cl", "lg", "lq"))
    for t in range(SIDE):
        rows = slice(t * TILE, (t + 1) * TILE)
        keep = pattern[tile_row + t, tile_col].astype(jnp.float32)
        masked[rows] = (density[rows].astype(jnp.float32) * keep).astype(jnp.bfloat16)
        count[t] = 0
    row = lax.broadcasted_iota(jnp.int32, (SIDE, TILE), 0)
    lane = lax.broadcasted_iota(jnp.int32, (SIDE, TILE), 1)
    places = jnp.zeros((SIDE, TILE), jnp.int32)
    for k in range(SIDE):
        loads[k].wait()

        def one(i, places, k=k):
            index = k * per + i
            owner = owners[index]
            r = owner // SIDE
            c = owner - r * SIDE
            pos = count[r]
            count[r] = pos + 1

            @pl.when(pos < CAP)
            def _():
                at = pl.ds(pl.multiple_of(pos * TILE, TILE), TILE)
                pltpu.make_async_copy(data.at[index], out.at[r, at], sem).start()

            @pl.when(pos >= CAP)
            def _():
                at = pl.ds(pl.multiple_of((pos - CAP) * TILE, TILE), TILE)
                pltpu.make_async_copy(data.at[index], rest.at[r, at], sem).start()

            here = (row == r) & (lane == pos)
            return jnp.where(here, c * SIDE + slots[index], places)

        places = lax.fori_loop(0, per, one, places, unroll=True)
    most = count[0]
    for r in range(1, SIDE):
        most = jnp.maximum(most, count[r])
    places = jnp.where(lane == FLAG, (most > CAP).astype(jnp.int32), places)
    for r in range(SIDE):
        places = jnp.where((row == r) & (lane == LAST), count[r], places)
    values = places.astype(jnp.float32)
    for r in range(SIDE):
        meta[r] = jnp.broadcast_to(values[r : r + 1], (META, TILE)).astype(jnp.bfloat16)
    tail = pltpu.make_async_copy(meta, out.at[:, pl.ds(BODY, META)], meta_sem)
    tail.start()
    tail.wait()
    pltpu.make_async_copy(data, data, sem).wait()


def pack(owners, slots, pattern, contributions, density):
    return pl.pallas_call(
        pack_kernel,
        out_shape=(
            jax.ShapeDtypeStruct((SIDE, BODY + META, TILE), jnp.bfloat16),
            jax.ShapeDtypeStruct((SIDE, REST * TILE, TILE), jnp.bfloat16),
            jax.ShapeDtypeStruct(density.shape, jnp.bfloat16),
        ),
        in_specs=[
            pl.BlockSpec(memory_space=pltpu.SMEM),
            pl.BlockSpec(memory_space=pltpu.SMEM),
            pl.BlockSpec(memory_space=pltpu.SMEM),
            pl.BlockSpec(memory_space=pl.ANY),
            pl.BlockSpec(memory_space=pltpu.VMEM),
        ],
        out_specs=(
            pl.BlockSpec(memory_space=pl.ANY),
            pl.BlockSpec(memory_space=pl.ANY),
            pl.BlockSpec(memory_space=pltpu.VMEM),
        ),
        scratch_shapes=[
            pltpu.VMEM(contributions.shape, jnp.bfloat16),
            pltpu.VMEM((SIDE, META, TILE), jnp.bfloat16),
            pltpu.SMEM((SIDE,), jnp.int32),
            pltpu.SemaphoreType.DMA((SIDE,)),
            pltpu.SemaphoreType.DMA,
            pltpu.SemaphoreType.DMA,
        ],
        compiler_params=pltpu.CompilerParams(vmem_limit_bytes=VMEM_MIB * MIB),
        cost_estimate=pl.CostEstimate(flops=0, bytes_accessed=7 * MIB, transcendentals=0),
        name="pack",
    )(owners, slots, pattern, contributions, density)


def combine_kernel(
    keeps, got, more, first, second, third, out, data, extra, meta, places, table, total, sems, meta_sem, table_sem, extra_sem
):
    head = pltpu.make_async_copy(got.at[:, pl.ds(BODY, META)], meta, meta_sem)
    head.start()
    loads = [
        pltpu.make_async_copy(got.at[r, pl.ds(0, BODY)], data.at[r], sems.at[r])
        for r in range(SIDE)
    ]
    for load in loads:
        load.start()
    total[...] = jnp.zeros_like(total)
    parity = lax.axis_index("cl")
    if not keeps:
        parity = 1 - parity
    head.wait()
    for r in range(SIDE):
        places[r : r + 1] = meta[r].astype(jnp.float32)[:1].astype(jnp.int32)
    listing = pltpu.make_async_copy(places, table, table_sem)
    listing.start()
    listing.wait()

    def put(place, values):
        column = place // SIDE

        @pl.when(column % 2 == parity)
        def _():
            at = column // 2 * SIDE + place % SIDE
            total[at] += values().astype(jnp.float32)

    for r in range(SIDE):
        loads[r].wait()
        held = table[r, LAST]

        def one(pos, carry, r=r):
            rows = pl.ds(pl.multiple_of(pos * TILE, TILE), TILE)
            put(table[r, pos], lambda: data[r, rows])
            return carry

        lax.fori_loop(0, jnp.minimum(held, CAP), one, 0)

        @pl.when(held > CAP)
        def _(r=r, held=held):
            load = pltpu.make_async_copy(more.at[r], extra, extra_sem)
            load.start()
            load.wait()

            def late(pos, carry):
                rows = pl.ds(pl.multiple_of(pos * TILE, TILE), TILE)
                put(table[r, CAP + pos], lambda: extra[rows])
                return carry

            lax.fori_loop(0, held - CAP, late, 0)

    def write(j, carry):
        for s in range(SIDE):
            columns = slice(s % 4 * TILE, (s % 4 + 1) * TILE)
            out[j, s // 4, :, columns] = total[j * SIDE + s].astype(jnp.bfloat16)
        return carry

    lax.fori_loop(0, SIDE // 2, write, 0)


def combine(keeps, got, more, *waits):
    return pl.pallas_call(
        functools.partial(combine_kernel, keeps),
        out_shape=jax.ShapeDtypeStruct((SIDE // 2, 2, TILE, SIDE * TILE // 2), jnp.bfloat16),
        in_specs=[pl.BlockSpec(memory_space=pl.ANY)] * 5,
        out_specs=pl.BlockSpec(memory_space=pltpu.VMEM),
        scratch_shapes=[
            pltpu.VMEM((SIDE, BODY, TILE), jnp.bfloat16),
            pltpu.VMEM((REST * TILE, TILE), jnp.bfloat16),
            pltpu.VMEM((SIDE, META, TILE), jnp.bfloat16),
            pltpu.VMEM((SIDE, TILE), jnp.int32),
            pltpu.SMEM((SIDE, TILE), jnp.int32),
            pltpu.VMEM((SIDE * SIDE // 2, TILE, TILE), jnp.float32),
            pltpu.SemaphoreType.DMA((SIDE,)),
            pltpu.SemaphoreType.DMA,
            pltpu.SemaphoreType.DMA,
            pltpu.SemaphoreType.DMA,
        ],
        compiler_params=pltpu.CompilerParams(vmem_limit_bytes=SMALL_MIB * MIB),
        cost_estimate=pl.CostEstimate(
            flops=2 * MIB, bytes_accessed=4 * MIB, transcendentals=0
        ),
        name="combine",
    )(got, more, *waits)


def add_kernel(keep, taken, first, second, out):
    out[...] = keep[...] + taken[...]


def add(keep, taken, *waits):
    return pl.pallas_call(
        add_kernel,
        out_shape=jax.ShapeDtypeStruct(keep.shape, keep.dtype),
        in_specs=[pl.BlockSpec(memory_space=pltpu.VMEM)] * 2 + [pl.BlockSpec(memory_space=pl.ANY)] * 2,
        out_specs=pl.BlockSpec(memory_space=pltpu.VMEM),
        compiler_params=pltpu.CompilerParams(vmem_limit_bytes=SMALL_MIB * MIB),
        cost_estimate=pl.CostEstimate(flops=MIB, bytes_accessed=3 * MIB, transcendentals=0),
        name="add",
    )(keep, taken, *waits)


def spread_kernel(parts, far, out):
    for half in range(2):
        rows = parts[0, half].astype(jnp.float32)
        for part in range(1, parts.shape[0]):
            rows += parts[part, half].astype(jnp.float32)
        rows = rows.astype(jnp.bfloat16)
        for chip in range(4):
            out[half * 4 + chip] = rows


def spread(parts, far):
    depth, width = parts.shape[2:]
    return pl.pallas_call(
        spread_kernel,
        out_shape=jax.ShapeDtypeStruct((SIDE, depth, width), jnp.bfloat16),
        in_specs=[pl.BlockSpec(memory_space=pltpu.VMEM), pl.BlockSpec(memory_space=pl.ANY)],
        out_specs=pl.BlockSpec(memory_space=pltpu.VMEM),
        compiler_params=pltpu.CompilerParams(vmem_limit_bytes=SMALL_MIB * MIB),
        cost_estimate=pl.CostEstimate(flops=MIB, bytes_accessed=2 * MIB, transcendentals=0),
        name="spread",
    )(parts, far)


def product_kernel(*refs):
    *parts, own, other, out, ham = refs
    half = SIDE * TILE
    core, layer = lax.axis_index("rc"), lax.axis_index("lq")
    column = lax.axis_index(("ch", "cl"))

    def slot(block):
        distance = (block - column + SIDE) % SIDE
        late = jnp.where(distance < 5, distance + 3, 10 - distance)
        return jnp.where(distance < 3, distance, late)

    @pl.when(pl.program_id(0) == 0)
    def _():
        for l in range(2):
            base = jnp.where(layer == l, 0, half)
            for j in range(SIDE // 2):
                mine = base + slot(2 * j + core) * TILE
                theirs = base + slot(2 * j + 1 - core) * TILE
                ham[pl.ds(pl.multiple_of(mine, TILE), TILE)] = own[l * 4 + j]
                ham[pl.ds(pl.multiple_of(theirs, TILE), TILE)] = other[l * 4 + j]

    rows = jnp.concatenate([part[c] for part in parts for c in range(part.shape[0])], axis=1)
    total = jnp.dot(rows, ham[...], preferred_element_type=jnp.float32)
    out[...] = total.astype(jnp.bfloat16)


def product_of(parts, own, other):
    rows = parts[0].shape[1]
    step = 256
    width = own.shape[2]
    blocks = [pl.BlockSpec((p.shape[0], step, TILE), lambda i: (0, i, 0)) for p in parts]
    whole = pl.BlockSpec(own.shape, lambda i: (0, 0, 0))
    return pl.pallas_call(
        product_kernel,
        out_shape=jax.ShapeDtypeStruct((rows, width), jnp.bfloat16),
        grid=(rows // step,),
        in_specs=[*blocks, whole, whole],
        out_specs=pl.BlockSpec((step, width), lambda i: (i, 0)),
        scratch_shapes=[pltpu.VMEM((2 * SIDE * TILE, width), jnp.bfloat16)],
        compiler_params=pltpu.CompilerParams(vmem_limit_bytes=SMALL_MIB * MIB),
        cost_estimate=pl.CostEstimate(
            flops=4 * rows * rows * width, bytes_accessed=7 * MIB, transcendentals=0
        ),
        name="product",
    )(*parts, own, other)


def finish_kernel(pattern, terms, out):
    tile_row = lax.axis_index(("rx", "rc", "lg", "lq"))
    tile_col = lax.axis_index(("ch", "cl")) * SIDE
    for t in range(SIDE):
        columns = slice(t % 4 * TILE, (t % 4 + 1) * TILE)
        total = jnp.zeros((TILE, TILE), jnp.float32)
        for group in range(4):
            total += terms[group * 2 + t // 4, :, columns].astype(jnp.float32)
        keep = pattern[tile_row, tile_col + t].astype(jnp.float32)
        out[:, t * TILE : (t + 1) * TILE] = (total * keep).astype(jnp.bfloat16)


def finish(pattern, terms):
    return pl.pallas_call(
        finish_kernel,
        out_shape=jax.ShapeDtypeStruct((TILE, SIDE * TILE), jnp.bfloat16),
        in_specs=[
            pl.BlockSpec(memory_space=pltpu.SMEM),
            pl.BlockSpec(memory_space=pltpu.VMEM),
        ],
        out_specs=pl.BlockSpec(memory_space=pltpu.VMEM),
        compiler_params=pltpu.CompilerParams(vmem_limit_bytes=SMALL_MIB * MIB),
        cost_estimate=pl.CostEstimate(flops=MIB, bytes_accessed=2 * MIB, transcendentals=0),
        name="finish",
    )(pattern, terms)


def exchange(values, axes):
    return lax.all_to_all(values, axes, split_axis=0, concat_axis=0, tiled=True)


def body(density, contributions, owners, slots, pattern):
    packed, rest, sparse = pack(owners.reshape(-1), slots, pattern, contributions, density)
    got = exchange(packed, ("rx", "rc"))

    def ahead(block, distance):
        return lax.ppermute(
            block, ("ch", "cl"), [(c, (c - distance) % SIDE) for c in range(SIDE)]
        )

    one, last, two, sixth = (ahead(sparse, distance) for distance in (1, -1, 2, -2))
    three, fifth = ahead(two, 1), ahead(sixth, -1)
    down = [(c, (c - 2) % SIDE) for c in range(SIDE)]
    up = [(SIDE + c, SIDE + (c + 2) % SIDE) for c in range(SIDE)]
    opposite = jnp.where(lax.axis_index("rc") == 0, two, sixth)
    four = lax.ppermute(opposite, ("rc", "ch", "cl"), down + up)
    swap = [(0, 1), (1, 0)]
    near = jnp.stack([sparse, one, two, last])
    far = lax.ppermute(near, "lq", swap)
    near_mid = sixth[None]
    far_mid = lax.ppermute(near_mid, "lq", swap)
    near_late = jnp.stack([fifth, three, four])
    far_late = lax.ppermute(near_late, "lq", swap)

    anyone = jnp.max(got[:, BODY, FLAG].astype(jnp.float32)) > 0
    more = lax.cond(anyone, lambda v: exchange(v, ("rx", "rc")), lambda v: v, rest)
    send = combine(False, got, more, three, four, fifth)
    count = SIDE
    even = [(c, c ^ 1) for c in range(count)]
    odd = [(count + c, count + (c + (1 if c % 2 else -1)) % count) for c in range(count)]
    taken = lax.ppermute(send, ("rc", "ch", "cl"), even + odd)
    keep = combine(True, got, more, near, near_late, near_late)
    parts = exchange(add(keep, taken, far, far_mid), "ch")

    own = exchange(spread(parts, far_late), ("lq", "rx"))
    other = lax.ppermute(own, "rc", swap)
    term = product_of((near, near_mid, near_late, far, far_mid, far_late), own, other)
    terms = exchange(term.reshape(SIDE, TILE, -1), ("lg", "lq"))
    return finish(pattern, terms)


def solution(mesh):
    layers, grid_rows, grid_cols = mesh.devices.shape
    split = Mesh(
        mesh.devices.reshape(layers // 2, 2, grid_rows // 2, 2, grid_cols // 2, 2),
        ("lg", "lq", "rx", "rc", "ch", "cl"),
    )
    layer, row, col = ("lg", "lq"), ("rx", "rc"), ("ch", "cl")
    return jax.shard_map(
        body,
        mesh=split,
        in_specs=(
            P(row, (*col, *layer)),
            P((*layer, *row, *col), None, None),
            P((*layer, *row, *col), None),
            P((*layer, *row, *col)),
            P(),
        ),
        out_specs=P((*row, *layer), col),
        check_vma=False,
    )
```

```python
import functools

import jax
import jax.numpy as jnp
from jax import lax
from jax.experimental import pallas as pl
from jax.experimental.pallas import tpu as pltpu
from jax.sharding import Mesh, PartitionSpec as P

TILE = 128
SIDE = 8
CAP = 12
REST = 4
BODY = CAP * TILE
META = 16
LAST = TILE - 1
FLAG = TILE - 2
MIB = 1 << 20
VMEM_MIB = 60
SMALL_MIB = 20


def pack_kernel(
    owners, slots, pattern, contributions, density, out, rest, masked, data, meta, count, sems, sem, meta_sem
):
    per = contributions.shape[0] // SIDE
    loads = [
        pltpu.make_async_copy(
            contributions.at[pl.ds(k * per, per)], data.at[pl.ds(k * per, per)], sems.at[k]
        )
        for k in range(SIDE)
    ]
    for load in loads:
        load.start()
    tile_row = lax.axis_index(("rx", "rc")) * SIDE
    tile_col = lax.axis_index(("ch", "cl", "lg", "lq"))
    for t in range(SIDE):
        rows = slice(t * TILE, (t + 1) * TILE)
        keep = pattern[tile_row + t, tile_col].astype(jnp.float32)
        masked[rows] = (density[rows].astype(jnp.float32) * keep).astype(jnp.bfloat16)
        count[t] = 0
    row = lax.broadcasted_iota(jnp.int32, (SIDE, TILE), 0)
    lane = lax.broadcasted_iota(jnp.int32, (SIDE, TILE), 1)
    places = jnp.zeros((SIDE, TILE), jnp.int32)
    for k in range(SIDE):
        loads[k].wait()

        def one(i, places, k=k):
            index = k * per + i
            owner = owners[index]
            r = owner // SIDE
            c = owner - r * SIDE
            pos = count[r]
            count[r] = pos + 1

            @pl.when(pos < CAP)
            def _():
                at = pl.ds(pl.multiple_of(pos * TILE, TILE), TILE)
                pltpu.make_async_copy(data.at[index], out.at[r, at], sem).start()

            @pl.when(pos >= CAP)
            def _():
                at = pl.ds(pl.multiple_of((pos - CAP) * TILE, TILE), TILE)
                pltpu.make_async_copy(data.at[index], rest.at[r, at], sem).start()

            here = (row == r) & (lane == pos)
            return jnp.where(here, c * SIDE + slots[index], places)

        places = lax.fori_loop(0, per, one, places, unroll=True)
    most = count[0]
    for r in range(1, SIDE):
        most = jnp.maximum(most, count[r])
    places = jnp.where(lane == FLAG, (most > CAP).astype(jnp.int32), places)
    for r in range(SIDE):
        places = jnp.where((row == r) & (lane == LAST), count[r], places)
    values = places.astype(jnp.float32)
    for r in range(SIDE):
        meta[r] = jnp.broadcast_to(values[r : r + 1], (META, TILE)).astype(jnp.bfloat16)
    tail = pltpu.make_async_copy(meta, out.at[:, pl.ds(BODY, META)], meta_sem)
    tail.start()
    tail.wait()
    pltpu.make_async_copy(data, data, sem).wait()


def pack(owners, slots, pattern, contributions, density):
    return pl.pallas_call(
        pack_kernel,
        out_shape=(
            jax.ShapeDtypeStruct((SIDE, BODY + META, TILE), jnp.bfloat16),
            jax.ShapeDtypeStruct((SIDE, REST * TILE, TILE), jnp.bfloat16),
            jax.ShapeDtypeStruct(density.shape, jnp.bfloat16),
        ),
        in_specs=[
            pl.BlockSpec(memory_space=pltpu.SMEM),
            pl.BlockSpec(memory_space=pltpu.SMEM),
            pl.BlockSpec(memory_space=pltpu.SMEM),
            pl.BlockSpec(memory_space=pl.ANY),
            pl.BlockSpec(memory_space=pltpu.VMEM),
        ],
        out_specs=(
            pl.BlockSpec(memory_space=pl.ANY),
            pl.BlockSpec(memory_space=pl.ANY),
            pl.BlockSpec(memory_space=pltpu.VMEM),
        ),
        scratch_shapes=[
            pltpu.VMEM(contributions.shape, jnp.bfloat16),
            pltpu.VMEM((SIDE, META, TILE), jnp.bfloat16),
            pltpu.SMEM((SIDE,), jnp.int32),
            pltpu.SemaphoreType.DMA((SIDE,)),
            pltpu.SemaphoreType.DMA,
            pltpu.SemaphoreType.DMA,
        ],
        compiler_params=pltpu.CompilerParams(vmem_limit_bytes=VMEM_MIB * MIB),
        cost_estimate=pl.CostEstimate(flops=0, bytes_accessed=7 * MIB, transcendentals=0),
        name="pack",
    )(owners, slots, pattern, contributions, density)


def combine_kernel(
    keeps, got, more, first, second, third, out, data, extra, meta, places, table, total, sems, meta_sem, table_sem, extra_sem
):
    head = pltpu.make_async_copy(got.at[:, pl.ds(BODY, META)], meta, meta_sem)
    head.start()
    loads = [
        pltpu.make_async_copy(got.at[r, pl.ds(0, BODY)], data.at[r], sems.at[r])
        for r in range(SIDE)
    ]
    for load in loads:
        load.start()
    total[...] = jnp.zeros_like(total)
    parity = lax.axis_index("cl")
    if not keeps:
        parity = 1 - parity
    head.wait()
    for r in range(SIDE):
        places[r : r + 1] = meta[r].astype(jnp.float32)[:1].astype(jnp.int32)
    listing = pltpu.make_async_copy(places, table, table_sem)
    listing.start()
    listing.wait()

    def put(place, values):
        column = place // SIDE

        @pl.when(column % 2 == parity)
        def _():
            at = column // 2 * SIDE + place % SIDE
            total[at] += values().astype(jnp.float32)

    for r in range(SIDE):
        loads[r].wait()
        held = table[r, LAST]

        def one(pos, carry, r=r):
            rows = pl.ds(pl.multiple_of(pos * TILE, TILE), TILE)
            put(table[r, pos], lambda: data[r, rows])
            return carry

        lax.fori_loop(0, jnp.minimum(held, CAP), one, 0)

        @pl.when(held > CAP)
        def _(r=r, held=held):
            load = pltpu.make_async_copy(more.at[r], extra, extra_sem)
            load.start()
            load.wait()

            def late(pos, carry):
                rows = pl.ds(pl.multiple_of(pos * TILE, TILE), TILE)
                put(table[r, CAP + pos], lambda: extra[rows])
                return carry

            lax.fori_loop(0, held - CAP, late, 0)

    def write(j, carry):
        for s in range(SIDE):
            columns = slice(s % 4 * TILE, (s % 4 + 1) * TILE)
            out[j, s // 4, :, columns] = total[j * SIDE + s].astype(jnp.bfloat16)
        return carry

    lax.fori_loop(0, SIDE // 2, write, 0)


def combine(keeps, got, more, *waits):
    return pl.pallas_call(
        functools.partial(combine_kernel, keeps),
        out_shape=jax.ShapeDtypeStruct((SIDE // 2, 2, TILE, SIDE * TILE // 2), jnp.bfloat16),
        in_specs=[pl.BlockSpec(memory_space=pl.ANY)] * 5,
        out_specs=pl.BlockSpec(memory_space=pltpu.VMEM),
        scratch_shapes=[
            pltpu.VMEM((SIDE, BODY, TILE), jnp.bfloat16),
            pltpu.VMEM((REST * TILE, TILE), jnp.bfloat16),
            pltpu.VMEM((SIDE, META, TILE), jnp.bfloat16),
            pltpu.VMEM((SIDE, TILE), jnp.int32),
            pltpu.SMEM((SIDE, TILE), jnp.int32),
            pltpu.VMEM((SIDE * SIDE // 2, TILE, TILE), jnp.float32),
            pltpu.SemaphoreType.DMA((SIDE,)),
            pltpu.SemaphoreType.DMA,
            pltpu.SemaphoreType.DMA,
            pltpu.SemaphoreType.DMA,
        ],
        compiler_params=pltpu.CompilerParams(vmem_limit_bytes=SMALL_MIB * MIB),
        cost_estimate=pl.CostEstimate(
            flops=2 * MIB, bytes_accessed=4 * MIB, transcendentals=0
        ),
        name="combine",
    )(got, more, *waits)


def add_kernel(keep, taken, wait, out):
    out[...] = keep[...] + taken[...]


def add(keep, taken, wait):
    return pl.pallas_call(
        add_kernel,
        out_shape=jax.ShapeDtypeStruct(keep.shape, keep.dtype),
        in_specs=[pl.BlockSpec(memory_space=pltpu.VMEM)] * 2 + [pl.BlockSpec(memory_space=pl.ANY)],
        out_specs=pl.BlockSpec(memory_space=pltpu.VMEM),
        compiler_params=pltpu.CompilerParams(vmem_limit_bytes=SMALL_MIB * MIB),
        cost_estimate=pl.CostEstimate(flops=MIB, bytes_accessed=3 * MIB, transcendentals=0),
        name="add",
    )(keep, taken, wait)


def spread_kernel(parts, far, out):
    for half in range(2):
        rows = parts[0, half].astype(jnp.float32)
        for part in range(1, parts.shape[0]):
            rows += parts[part, half].astype(jnp.float32)
        rows = rows.astype(jnp.bfloat16)
        for chip in range(4):
            out[half * 4 + chip] = rows


def spread(parts, far):
    depth, width = parts.shape[2:]
    return pl.pallas_call(
        spread_kernel,
        out_shape=jax.ShapeDtypeStruct((SIDE, depth, width), jnp.bfloat16),
        in_specs=[pl.BlockSpec(memory_space=pltpu.VMEM), pl.BlockSpec(memory_space=pl.ANY)],
        out_specs=pl.BlockSpec(memory_space=pltpu.VMEM),
        compiler_params=pltpu.CompilerParams(vmem_limit_bytes=SMALL_MIB * MIB),
        cost_estimate=pl.CostEstimate(flops=MIB, bytes_accessed=2 * MIB, transcendentals=0),
        name="spread",
    )(parts, far)


def product_kernel(*refs):
    *parts, own, other, out, ham = refs
    half = SIDE * TILE
    core, layer = lax.axis_index("rc"), lax.axis_index("lq")
    column = lax.axis_index(("ch", "cl"))

    def slot(block):
        distance = (block - column + SIDE) % SIDE
        late = jnp.where(distance < 5, distance + 3, 10 - distance)
        return jnp.where(distance < 3, distance, late)

    @pl.when(pl.program_id(0) == 0)
    def _():
        for l in range(2):
            base = jnp.where(layer == l, 0, half)
            for j in range(SIDE // 2):
                mine = base + slot(2 * j + core) * TILE
                theirs = base + slot(2 * j + 1 - core) * TILE
                ham[pl.ds(pl.multiple_of(mine, TILE), TILE)] = own[l * 4 + j]
                ham[pl.ds(pl.multiple_of(theirs, TILE), TILE)] = other[l * 4 + j]

    rows = jnp.concatenate([part[c] for part in parts for c in range(part.shape[0])], axis=1)
    total = jnp.dot(rows, ham[...], preferred_element_type=jnp.float32)
    out[...] = total.astype(jnp.bfloat16)


def product_of(parts, own, other):
    rows = parts[0].shape[1]
    step = 256
    width = own.shape[2]
    blocks = [pl.BlockSpec((p.shape[0], step, TILE), lambda i: (0, i, 0)) for p in parts]
    whole = pl.BlockSpec(own.shape, lambda i: (0, 0, 0))
    return pl.pallas_call(
        product_kernel,
        out_shape=jax.ShapeDtypeStruct((rows, width), jnp.bfloat16),
        grid=(rows // step,),
        in_specs=[*blocks, whole, whole],
        out_specs=pl.BlockSpec((step, width), lambda i: (i, 0)),
        scratch_shapes=[pltpu.VMEM((2 * SIDE * TILE, width), jnp.bfloat16)],
        compiler_params=pltpu.CompilerParams(vmem_limit_bytes=SMALL_MIB * MIB),
        cost_estimate=pl.CostEstimate(
            flops=4 * rows * rows * width, bytes_accessed=7 * MIB, transcendentals=0
        ),
        name="product",
    )(*parts, own, other)


def finish_kernel(pattern, terms, out):
    tile_row = lax.axis_index(("rx", "rc", "lg", "lq"))
    tile_col = lax.axis_index(("ch", "cl")) * SIDE
    for t in range(SIDE):
        columns = slice(t % 4 * TILE, (t % 4 + 1) * TILE)
        total = jnp.zeros((TILE, TILE), jnp.float32)
        for group in range(4):
            total += terms[group * 2 + t // 4, :, columns].astype(jnp.float32)
        keep = pattern[tile_row, tile_col + t].astype(jnp.float32)
        out[:, t * TILE : (t + 1) * TILE] = (total * keep).astype(jnp.bfloat16)


def finish(pattern, terms):
    return pl.pallas_call(
        finish_kernel,
        out_shape=jax.ShapeDtypeStruct((TILE, SIDE * TILE), jnp.bfloat16),
        in_specs=[
            pl.BlockSpec(memory_space=pltpu.SMEM),
            pl.BlockSpec(memory_space=pltpu.VMEM),
        ],
        out_specs=pl.BlockSpec(memory_space=pltpu.VMEM),
        compiler_params=pltpu.CompilerParams(vmem_limit_bytes=SMALL_MIB * MIB),
        cost_estimate=pl.CostEstimate(flops=MIB, bytes_accessed=2 * MIB, transcendentals=0),
        name="finish",
    )(pattern, terms)


def exchange(values, axes):
    return lax.all_to_all(values, axes, split_axis=0, concat_axis=0, tiled=True)


def body(density, contributions, owners, slots, pattern):
    packed, rest, sparse = pack(owners.reshape(-1), slots, pattern, contributions, density)
    got = exchange(packed, ("rx", "rc"))

    def ahead(block, distance):
        return lax.ppermute(
            block, ("ch", "cl"), [(c, (c - distance) % SIDE) for c in range(SIDE)]
        )

    one, last, two, sixth = (ahead(sparse, distance) for distance in (1, -1, 2, -2))
    three, fifth = ahead(two, 1), ahead(sixth, -1)
    down = [(c, (c - 2) % SIDE) for c in range(SIDE)]
    up = [(SIDE + c, SIDE + (c + 2) % SIDE) for c in range(SIDE)]
    opposite = jnp.where(lax.axis_index("rc") == 0, two, sixth)
    four = lax.ppermute(opposite, ("rc", "ch", "cl"), down + up)
    swap = [(0, 1), (1, 0)]
    near = jnp.stack([sparse, one, two, last, sixth])
    far = lax.ppermute(near, "lq", swap)
    near_late = jnp.stack([fifth, three, four])
    far_late = lax.ppermute(near_late, "lq", swap)

    anyone = jnp.max(got[:, BODY, FLAG].astype(jnp.float32)) > 0
    more = lax.cond(anyone, lambda v: exchange(v, ("rx", "rc")), lambda v: v, rest)
    send = combine(False, got, more, three, four, fifth)
    count = SIDE
    even = [(c, c ^ 1) for c in range(count)]
    odd = [(count + c, count + (c + (1 if c % 2 else -1)) % count) for c in range(count)]
    taken = lax.ppermute(send, ("rc", "ch", "cl"), even + odd)
    keep = combine(True, got, more, near, near_late, near_late)
    parts = exchange(add(keep, taken, far), "ch")

    own = exchange(spread(parts, far_late), ("lq", "rx"))
    other = lax.ppermute(own, "rc", swap)
    term = product_of((near, near_late, far, far_late), own, other)
    terms = exchange(term.reshape(SIDE, TILE, -1), ("lg", "lq"))
    return finish(pattern, terms)


def solution(mesh):
    layers, grid_rows, grid_cols = mesh.devices.shape
    split = Mesh(
        mesh.devices.reshape(layers // 2, 2, grid_rows // 2, 2, grid_cols // 2, 2),
        ("lg", "lq", "rx", "rc", "ch", "cl"),
    )
    layer, row, col = ("lg", "lq"), ("rx", "rc"), ("ch", "cl")
    return jax.shard_map(
        body,
        mesh=split,
        in_specs=(
            P(row, (*col, *layer)),
            P((*layer, *row, *col), None, None),
            P((*layer, *row, *col), None),
            P((*layer, *row, *col)),
            P(),
        ),
        out_specs=P((*row, *layer), col),
        check_vma=False,
    )
```
